32 devices in a mesh: sect: 4 (over z), dev: 8 (over y, x, core).
Axes of the slice: x: 2, y: 2, z: 4, core: 2. Of those that a mesh axis runs over, the one named last changes fastest.
Arguments:
- points: float32 [3, 524288], P(None, ('sect', 'dev')), may hold values from 0 to 1
- vectors: bfloat16 [8, 524288], P(None, ('sect', 'dev')), may hold values from -6 to 6
- near_list: int32 [2048, 16], P(('sect', 'dev')), may hold values from 0 to 2047, as said below
- near_count: int32 [2048], P(('sect', 'dev')), may hold values from 1 to 16, as said below
- couple_list: int32 [2048, 16], P(('sect', 'dev')), may hold values from 0 to 2047, as said below
- leaf_basis: bfloat16 [2048, 64, 256], P(('sect', 'dev')), may hold values from -0.375 to 0.375
- local_transfer: bfloat16 [32, 126, 4096], P(('sect', 'dev')), may hold values from -0.625 to 0.625
- couple_block: bfloat16 [2048, 16, 4096], P(('sect', 'dev')), may hold values from -0.1875 to 0.1875
- upper_transfer: bfloat16 [64, 4096], P(('sect', 'dev')), may hold values from -0.625 to 0.625
- upper_couple: bfloat16 [64, 3, 4096], P(('sect', 'dev')), may hold values from -0.4375 to 0.4375
Outputs:
- product: float32 [8, 524288], P(None, ('sect', 'dev'))
The draws below stay inside these ranges and needn't reach their ends.
Inputs may be any that keep to these rules, and one draw needn't show every extreme that they name: `near_list`: row l names 16 different leaves other than l, each held by the device that holds l or by one of the two devices next to it in the order of devices. The leading near_count[l] entries of row l of near_list are the near-field partners of leaf l. `couple_list`: row l names 16 different leaves other than l, each held by a device at most 2 places from the one that holds l in the order of devices.
All inputs are finite; a program needn't handle non-finite values.
Results may differ from the reference program's by a relative error of at most 0.03.
Values may be sent and summed in bfloat16 or wider, within the bound.
No kernel may reach another device: no remote copies, remote signals or barrier semaphores. Data moves between devices by JAX's collectives and lax.ppermute only.
A program may use at most 128 MiB of HBM per device.

```python
import math
import jax
import jax.numpy as jnp
from jax import lax

LEAF = 256
RANK = 64
VEC = 8
LEAVES_DEV = 64
NEAR = 16
COUPLE = 16
REACH = 2
LEAVES = 2048
NPTS = 524288
DEVICES = 32


def window_pick(key, before, after, wanted):
    leaf_ids = jnp.arange(LEAVES, dtype=jnp.int32)
    owner_dev = leaf_ids // LEAVES_DEV
    window_width = (before + after + 1) * LEAVES_DEV
    offsets = jnp.arange(window_width, dtype=jnp.int32)
    candidate = (owner_dev - before)[:, None] * LEAVES_DEV + offsets[None, :]
    usable = (candidate >= 0) & (candidate < LEAVES) & (candidate != leaf_ids[:, None])
    scores = jax.random.randint(key, (LEAVES, window_width), 0, 1 << 20, dtype=jnp.int32) * window_width + offsets[None, :]
    scores = jnp.where(usable, scores, -1)
    _, chosen = lax.top_k(scores, wanted)
    return jnp.take_along_axis(candidate, chosen, axis=1).astype(jnp.int32)


def draw_near_list(key, part):
    key = jax.random.fold_in(key, 1)
    return window_pick(key, 1, 1, NEAR)


def draw_couple_list(key, part):
    key = jax.random.fold_in(key, 2)
    return window_pick(key, REACH, REACH, COUPLE)


def draw_near_count(key, part):
    key = jax.random.fold_in(key, 3)
    key_crowded, key_sparse, key_leaf = jax.random.split(key, 3)
    crowded = jax.random.randint(key_crowded, (DEVICES,), 0, 8, dtype=jnp.int32) == 0
    sparse_level = jax.random.randint(key_sparse, (DEVICES,), max(NEAR // 4, 1), NEAR // 2 + 1, dtype=jnp.int32)
    device_level = jnp.where(crowded, NEAR, sparse_level)
    device_level = jnp.where(jnp.arange(DEVICES) == 0, NEAR, device_level)
    owner_dev = jnp.arange(LEAVES, dtype=jnp.int32) // LEAVES_DEV
    counts = jnp.maximum(device_level[owner_dev] - jax.random.randint(key_leaf, (LEAVES,), 0, 2, dtype=jnp.int32), 1)
    counts = jnp.where(jnp.arange(LEAVES) == 0, NEAR, counts)
    return counts.astype(jnp.int32)


def steps_of(rng, extent, pieces, low, high):
    loudness, own = 1.0, jax.random.fold_in(rng, 6)
    for dim, shards_of in pieces:
        draws = jnp.exp(jax.random.uniform(jax.random.fold_in(own, dim), (shards_of,), jnp.float32, low / len(pieces), high / len(pieces)))
        loudness = loudness * jnp.repeat(draws, extent[dim] // shards_of).reshape([-1 if axis == dim else 1 for axis in range(len(extent))])
    return loudness


def bell_draw(key, extent, width, bound, cuts=(), kind=jnp.bfloat16):
    result = width * jax.random.normal(key, extent, jnp.float32)
    if cuts:
        result = result * steps_of(key, extent, cuts, -0.22, 0.18)
    return jnp.clip(result, -bound, bound).astype(kind)


def setup_inputs(seed: int = 0) -> dict:
    arg_keys = jax.random.split(jax.random.key(seed), 11)
    return {
        "points": jnp.clip(1.0 * jax.random.uniform(arg_keys[0], (3, NPTS), jnp.float32) ** steps_of(arg_keys[0], (3, NPTS), ((1, 32),), -0.2, 0.2), 0.0, 1.0),
        "vectors": bell_draw(arg_keys[1], (VEC, NPTS), 1.0, 6.0, ((1, 32),)),
        "near_list": draw_near_list(jax.random.fold_in(arg_keys[10], 71), 0),
        "near_count": draw_near_count(jax.random.fold_in(arg_keys[10], 71), 0),
        "couple_list": draw_couple_list(jax.random.fold_in(arg_keys[10], 71), 0),
        "leaf_basis": bell_draw(arg_keys[5], (LEAVES, RANK, LEAF), LEAF ** -0.5, 0.375, ((0, 32),)),
        "local_transfer": bell_draw(arg_keys[6], (DEVICES, 2 * LEAVES_DEV - 2, RANK * RANK), (RANK * 3 // 2) ** -0.5, 0.625, ((0, 32),)),
        "couple_block": bell_draw(arg_keys[7], (LEAVES, COUPLE, RANK * RANK), (COUPLE * RANK) ** -0.5, 0.1875, ((0, 32),)),
        "upper_transfer": bell_draw(arg_keys[8], (2 * DEVICES, RANK * RANK), (RANK * 3 // 2) ** -0.5, 0.625, ((0, 32),)),
        "upper_couple": bell_draw(arg_keys[9], (2 * DEVICES, 3, RANK * RANK), (3 * RANK) ** -0.5, 0.4375, ((0, 32),)),
    }


soft_sq = 0.0025
even_offsets = (-2, 2, 3)
odd_offsets = (-3, -2, 2)
highest = lax.Precision.HIGHEST

def batched(left, right):
    return jnp.einsum('nvr,nrs->nvs', left.astype(jnp.float32), right.astype(jnp.float32), precision=highest)

def batched_back(left, right):
    return jnp.einsum('nvs,nrs->nvr', left.astype(jnp.float32), right.astype(jnp.float32), precision=highest)

def partner_terms(level_top, blocks):
    node_count = level_top.shape[0]
    node_index = jnp.arange(node_count, dtype=jnp.int32)
    is_odd = node_index % 2 == 1
    summed = jnp.zeros(level_top.shape, jnp.float32)
    for slot_index in range(3):
        offset = jnp.where(is_odd, odd_offsets[slot_index], even_offsets[slot_index]).astype(jnp.int32)
        partner = node_index + offset
        in_range = (partner >= 0) & (partner < node_count)
        source = jnp.take(level_top, jnp.clip(partner, 0, node_count - 1), axis=0)
        update = batched(source, blocks[:, slot_index])
        summed = summed + jnp.where(in_range[:, None, None], update, 0.0)
    return summed

def top_tree(device_coef, upper_mats, upper_blocks, top_levels):
    devices = device_coef.shape[0]
    top_chain = [device_coef]
    for up_step in range(1, top_levels):
        node_count = devices >> up_step - 1
        product = batched(top_chain[-1], upper_mats[node_count:2 * node_count])
        top_chain.append((product[0::2] + product[1::2]).astype(jnp.bfloat16))
    parent = jnp.zeros((1,) + device_coef.shape[1:], jnp.bfloat16)
    for tree_level in range(top_levels - 1, -1, -1):
        node_count = devices >> tree_level
        doubled = jnp.repeat(parent, 2, axis=0)
        update = batched_back(doubled, upper_mats[node_count:2 * node_count])
        update = update + partner_terms(top_chain[tree_level], upper_blocks[node_count:2 * node_count])
        parent = update.astype(jnp.bfloat16)
    return parent

def kernel_block(source, target, kernel_scale):
    delta_x = source[0][:, :, None] - target[0][:, None, :]
    delta_y = source[1][:, :, None] - target[1][:, None, :]
    delta_z = source[2][:, :, None] - target[2][:, None, :]
    distance_sq = delta_x * delta_x + delta_y * delta_y + delta_z * delta_z
    return (lax.rsqrt(distance_sq + soft_sq) * kernel_scale).astype(jnp.bfloat16)

def near_product(source_vectors, kernel):
    return jnp.einsum('vnq,nqp->vnp', source_vectors.astype(jnp.float32), kernel.astype(jnp.float32), precision=highest)

def reference(points, vectors, near_list, near_count, couple_list, leaf_basis, local_transfer, couple_block, upper_transfer, upper_couple):
    levels = LEAVES_DEV.bit_length() - 1
    top_levels = DEVICES.bit_length() - 1
    leaf_vectors = vectors.reshape(VEC, LEAVES, LEAF)
    coefficients = jnp.einsum('vlp,lrp->lvr', leaf_vectors.astype(jnp.float32), leaf_basis.astype(jnp.float32), precision=highest).astype(jnp.bfloat16)
    transfers = local_transfer.reshape(DEVICES, 2 * LEAVES_DEV - 2, RANK, RANK)
    up_chain = [coefficients]
    for tree_level in range(levels):
        level_width = LEAVES_DEV >> tree_level
        slot_start = 2 * LEAVES_DEV - 2 * level_width
        matrices = transfers[:, slot_start:slot_start + level_width].reshape(DEVICES * level_width, RANK, RANK)
        product = batched(up_chain[-1], matrices)
        up_chain.append((product[0::2] + product[1::2]).astype(jnp.bfloat16))
    device_down = top_tree(up_chain[-1], upper_transfer.reshape(2 * DEVICES, RANK, RANK), upper_couple.reshape(2 * DEVICES, 3, RANK, RANK), top_levels)
    blocks = couple_block.reshape(DEVICES, LEAVES_DEV, COUPLE, RANK, RANK)
    partner_ids = couple_list.reshape(DEVICES, LEAVES_DEV, COUPLE)

    def couple_one(packed):
        ids_here, blocks_here = packed
        partners = jnp.take(coefficients, ids_here.reshape(-1), axis=0).reshape(LEAVES_DEV, COUPLE, VEC, RANK)
        return jnp.einsum('lsvr,lsrt->lvt', partners.astype(jnp.float32), blocks_here.astype(jnp.float32), precision=highest)
    couple_sum = lax.map(couple_one, (partner_ids, blocks)).reshape(LEAVES, VEC, RANK)
    parent = device_down
    for tree_level in range(levels - 1, -1, -1):
        level_width = LEAVES_DEV >> tree_level
        slot_start = 2 * LEAVES_DEV - 2 * level_width
        matrices = transfers[:, slot_start:slot_start + level_width].reshape(DEVICES * level_width, RANK, RANK)
        update = batched_back(jnp.repeat(parent, 2, axis=0), matrices)
        if tree_level == 0:
            update = update + couple_sum
        parent = update.astype(jnp.bfloat16)
    far_field = jnp.einsum('lvr,lrp->vlp', parent.astype(jnp.float32), leaf_basis.astype(jnp.float32), precision=highest)
    points_leaf = points.reshape(3, LEAVES, LEAF)
    kernel_scale = 1.0 / math.sqrt(LEAF * (NEAR + 1))

    def near_one(packed):
        ids_here, counts_here, device = packed
        own_ids = device * LEAVES_DEV + jnp.arange(LEAVES_DEV, dtype=jnp.int32)
        own_points = jnp.take(points_leaf, own_ids, axis=1)
        own_vectors = jnp.take(leaf_vectors, own_ids, axis=1)
        self_term = near_product(own_vectors, kernel_block(own_points, own_points, kernel_scale))

        def add_slot(slot_index, running):
            column = lax.dynamic_slice_in_dim(ids_here, slot_index, 1, 1)[:, 0]
            source_points = jnp.take(points_leaf, column, axis=1)
            source_vectors = jnp.take(leaf_vectors, column, axis=1)
            update = near_product(source_vectors, kernel_block(source_points, own_points, kernel_scale))
            live_slot = (slot_index < counts_here)[None, :, None]
            return running + jnp.where(live_slot, update, 0.0)
        return lax.fori_loop(0, NEAR, add_slot, self_term)
    near_field = lax.map(near_one, (near_list.reshape(DEVICES, LEAVES_DEV, NEAR), near_count.reshape(DEVICES, LEAVES_DEV), jnp.arange(DEVICES, dtype=jnp.int32)))
    near_field = jnp.transpose(near_field, (1, 0, 2, 3)).reshape(VEC, LEAVES, LEAF)
    return (far_field + near_field).reshape(VEC, NPTS)
```

```python
import math

import jax
import jax.numpy as jnp
import numpy as np
from jax import lax
from jax.experimental import pallas as pl
from jax.experimental.pallas import tpu as pltpu
from jax.sharding import PartitionSpec as P

REACH = 2
AXES = ("sect", "dev")
UNROLL = 8
VMEM_BYTES = 58 * 1024 * 1024

soft_sq = 0.0025
even_offsets = (-2, 2, 3)
odd_offsets = (-3, -2, 2)


def from_behind(block, distance):
    devices = range(lax.axis_size(AXES))
    route = [(i - distance, i) for i in devices if i - distance in devices]
    return lax.ppermute(block, AXES, route)


def feature_maps():
    source = np.zeros((32, 16), np.float32)
    target = np.zeros((32, 16), np.float32)
    coords = np.zeros((8, 16), np.float32)
    for c in range(3):
        hi, mid = 8 + c, 11 + c
        source[c, hi] = source[3 + c, hi] = 1.0
        source[6 + c, mid] = source[9 + c, mid] = 1.0
        target[c, hi] = target[6 + c, hi] = -2.0
        target[3 + c, mid] = target[9 + c, mid] = -2.0
        coords[c, hi] = coords[c, mid] = 1.0
    source[15:18, 14] = 1.0
    target[12:15, 14] = 1.0
    return source, coords, target


def split3(x):
    a = x.astype(jnp.bfloat16).astype(jnp.float32)
    b = (x - a).astype(jnp.bfloat16).astype(jnp.float32)
    c = (x - a - b).astype(jnp.bfloat16).astype(jnp.float32)
    return a, b, c


def flow(a, b, only):
    gap = a - b
    return jnp.where((a > 0) & (b > 0) & (gap > 24), (gap * jnp.where(only, 128, 85)) >> 8, 0)


def near_kernel(
    devices,
    place_ref,
    low_bit,
    maps_ref,
    weights_ref,
    left_ref,
    own_ref,
    right_ref,
    left_out,
    own_out,
    right_out,
    s_own,
    s_side,
    t_ref,
    v_own,
    v_side,
    g_even,
    g_odd,
    sum_ref,
    masks_v,
    ids_v,
    masks,
    ids,
    sems,
):
    leaves = own_ref.shape[1] // 256
    slots = weights_ref.shape[0] // leaves
    kernel_scale = 1.0 / math.sqrt(256 * (slots + 1))
    row = lax.broadcasted_iota(jnp.int32, (8, 2048), 0)
    zero = jnp.int32(0)
    f32 = jnp.float32

    def listed(ref):
        return ref[8:16, 0 : leaves * slots].astype(f32)[7:8]

    def band(x, k):
        return jnp.where((x > leaves * k) & (x <= leaves * (k + 1)), 1.0, 0.0)

    mine, theirs_l, theirs_r = listed(own_ref), listed(left_ref), listed(right_ref)
    flags = [band(mine, 1), band(mine, 0), band(mine, 2), band(theirs_l, 2), band(theirs_r, 0)]
    flags += [jnp.where(x > 0.0, 1.0, 0.0) for x in (mine, theirs_l, theirs_r)]
    flags = jnp.concatenate(flags, axis=0).astype(jnp.bfloat16)
    masks_v[...] = jnp.dot(flags, weights_ref[...], preferred_element_type=f32).astype(jnp.int32)
    places = [mine - (leaves + 1.0), theirs_l - (2 * leaves + 1.0), theirs_r - 1.0]
    places += [jnp.zeros((5, leaves * slots), f32)]
    ids_v[...] = jnp.concatenate(places, axis=0).astype(jnp.int32)
    masks_copy = pltpu.make_async_copy(masks_v, masks, sems.at[0])
    ids_copy = pltpu.make_async_copy(ids_v, ids, sems.at[1])
    masks_copy.start()
    ids_copy.start()

    def put_source(ref, chunk, s_ref, v_ref, leaf, target):
        block = ref[:, pl.ds(pl.multiple_of(chunk * 2048, 2048), 2048)]
        wide = jnp.dot(maps_ref[...], block, preferred_element_type=f32)
        coord = wide[32:40]
        norm = jnp.sum(coord * coord, axis=0, keepdims=True)
        a, b, c = split3(norm)
        mixed = jnp.where(row == 7, 1.0, wide[8:16])
        mixed = jnp.where(row == 4, a, jnp.where(row == 5, b, jnp.where(row == 6, c, mixed)))
        rows = jnp.concatenate([wide[0:8], mixed, wide[16:32]], axis=0).astype(jnp.bfloat16)
        for half in range(2):
            quad = [rows[:, 256 * k : 256 * k + 256] for k in range(4 * half, 4 * half + 4)]
            turned = jnp.concatenate(quad, axis=0).T
            for k in range(4):
                s_ref[leaf + 4 * half + k] = turned[:, 32 * k : 32 * k + 32]
        for k in range(8):
            v_ref[leaf + k] = block[:, 256 * k : 256 * k + 256]
        a, b, c = split3(norm + soft_sq)
        first = jnp.where(row == 7, a, wide[48:56])
        second = jnp.where(row == 0, b, jnp.where(row == 1, c, wide[56:64]))
        rows = jnp.concatenate([wide[40:48], first, second, wide[64:72]], axis=0).astype(jnp.bfloat16)
        for k in range(8):
            t_ref[target + k] = rows[:, 256 * k : 256 * k + 256]

    def build_own(chunk, _):
        put_source(own_ref, chunk, s_own, v_own, chunk * 8, chunk * 8)
        return 0

    lax.fori_loop(0, leaves // 8, build_own, 0, unroll=4)
    v_own[leaves] = jnp.zeros((16, 256), jnp.bfloat16)
    v_side[2 * leaves] = jnp.zeros((16, 256), jnp.bfloat16)
    sum_ref[...] = jnp.zeros_like(sum_ref)
    masks_copy.wait()
    ids_copy.wait()

    def pairs(k):
        found = masks[k, 2 * leaves]
        return jnp.where(found > 0, found + leaves, 0)

    here, at_left, at_right = pairs(5), pairs(6), pairs(7)
    me = place_ref[0]

    def whole_rows(k, allowed):
        def fits(carry):
            t, total = carry
            return (t < leaves) & (total + masks[k, leaves + jnp.minimum(t, leaves - 1)] <= allowed)

        def step(carry):
            t, total = carry
            return t + 1, total + masks[k, leaves + t]

        rows, _ = lax.while_loop(fits, step, (jnp.where(allowed > 0, 0, leaves).astype(jnp.int32), zero))
        return jnp.where(allowed > 0, rows, 0)

    give_left = whole_rows(1, flow(here, at_left, at_right == 0))
    give_right = whole_rows(2, flow(here, at_right, at_left == 0))
    take_left = whole_rows(3, flow(at_left, here, me == 1))
    take_right = whole_rows(4, flow(at_right, here, me == devices - 2))

    def mask_of(at, own):
        if own:
            at = jnp.minimum(at, 3 * leaves - 1)
            k = jnp.where(at < leaves, 0, jnp.where(at < 2 * leaves, 3, 4))
            return masks[k, at & (leaves - 1)] | jnp.where(at < leaves, 1 << slots, 0)
        at = jnp.minimum(at, leaves - 1)
        return jnp.where(at < give_left, 0, masks[1, at]) | jnp.where(at < give_right, 0, masks[2, at])

    def after_row(at, own):
        if own:
            return jnp.where(at + 1 == leaves + take_left, 2 * leaves, at + 1)
        return at + 1

    def add_held(held, g_in, v_ref):
        return [jnp.dot(v_ref[held[u][0]], g_in[u], preferred_element_type=f32) for u in range(UNROLL)]

    def put_held(held, updates):
        for u in range(UNROLL):
            sum_ref[held[u][1]] += updates[u][0:8]

    def half(state, held, g_in, g_out, own, end):
        at, mask = state
        fresh = []
        s_ref, v_ref = (s_own, v_own) if own else (s_side, v_side)
        idle = leaves if own else 2 * leaves
        updates = add_held(held, g_in, v_ref)
        for u in range(UNROLL):
            active = at < end
            target = jnp.where(active, at, 0)
            low = mask & -mask
            slot = low_bit[lax.shift_right_logical(low * 0x077CB531, 27)]
            place = ids[target >> (leaves.bit_length() - 1), (target & (leaves - 1)) * slots + jnp.minimum(slot, slots - 1)]
            if own:
                source = jnp.where(slot == slots, target, place)
            else:
                source = jnp.where(place < 0, place + leaves, place)
            used = active & (low != 0)
            source = jnp.where(used, source, 0)
            fresh.append((jnp.where(used, source, idle), target))
            dist = jnp.dot(s_ref[source], t_ref[target], preferred_element_type=f32)
            g_out[u] = lax.rsqrt(dist.astype(jnp.bfloat16))
            rest = mask ^ low
            done = active & (rest == 0)
            following = after_row(at, own)
            mask = jnp.where(done, mask_of(following, own), jnp.where(active, rest, mask))
            at = jnp.where(done, following, at)
        put_held(held, updates)
        return (at, mask), tuple(fresh)

    def both(state, held, own, end):
        state, held = half(state, held, g_even, g_odd, own, end)
        return half(state, held, g_odd, g_even, own, end)

    def nothing(own):
        idle = leaves if own else 2 * leaves
        return tuple((jnp.int32(idle), zero) for _ in range(UNROLL))

    def first_bodies(chunk, carry):
        carry = both(*carry, True, leaves)
        put_source(left_ref, chunk, s_side, v_side, chunk * 8, leaves + chunk * 8)
        put_source(right_ref, chunk, s_side, v_side, leaves + chunk * 8, 2 * leaves + chunk * 8)
        return carry

    def run(own, end, state, held):
        def more(carry):
            return carry[0][0] < end

        state, held = lax.while_loop(more, lambda carry: both(*carry, own, end), (state, held))
        put_held(held, add_held(held, g_even, v_own if own else v_side))

    g_even[...] = jnp.zeros_like(g_even)
    state, held = lax.fori_loop(0, leaves // 8, first_bodies, ((zero, mask_of(zero, True)), nothing(True)))
    run(True, 2 * leaves + take_right, state, held)
    run(False, leaves, (zero, mask_of(zero, False)), nothing(False))

    def finish(chunk, _):
        for k in range(8):
            leaf = chunk * 8 + k
            cols = pl.ds(pl.multiple_of(leaf * 256, 256), 256)
            for side, ref in enumerate((own_out, left_out, right_out)):
                ref[:, cols] = sum_ref[side * leaves + leaf] * kernel_scale
        return 0

    lax.fori_loop(0, leaves // 8, finish, 0)


def near_field(devices, place, leaves, slots, left, own, right):
    points = own.shape[1]
    maps = jnp.asarray(np.concatenate(feature_maps(), axis=0), jnp.bfloat16)
    table = np.zeros((32,), np.int32)
    for bit in range(32):
        table[((0x077CB531 << bit) & 0xFFFFFFFF) >> 27] = bit
    weights = np.zeros((leaves * slots, 256), np.float32)
    for t in range(leaves):
        for k in range(slots):
            weights[t * slots + k, t] = 2.0**k
            weights[t * slots + k, leaves + t] = 1.0
    weights[:, 2 * leaves] = 1.0
    smem = pl.BlockSpec(memory_space=pltpu.SMEM)
    vmem = pl.BlockSpec(memory_space=pltpu.VMEM)
    return pl.pallas_call(
        lambda *refs: near_kernel(devices, *refs),
        out_shape=(jax.ShapeDtypeStruct((8, points), jnp.float32),) * 3,
        in_specs=[smem] * 2 + [vmem] * 5,
        out_specs=(vmem,) * 3,
        scratch_shapes=[
            pltpu.VMEM((leaves, 256, 32), jnp.bfloat16),
            pltpu.VMEM((2 * leaves, 256, 32), jnp.bfloat16),
            pltpu.VMEM((3 * leaves, 32, 256), jnp.bfloat16),
            pltpu.VMEM((leaves + 1, 16, 256), jnp.bfloat16),
            pltpu.VMEM((2 * leaves + 1, 16, 256), jnp.bfloat16),
            pltpu.VMEM((UNROLL, 256, 256), jnp.bfloat16),
            pltpu.VMEM((UNROLL, 256, 256), jnp.bfloat16),
            pltpu.VMEM((3 * leaves, 8, 256), jnp.float32),
            pltpu.VMEM((8, 256), jnp.int32),
            pltpu.VMEM((8, leaves * slots), jnp.int32),
            pltpu.SMEM((8, 256), jnp.int32),
            pltpu.SMEM((8, leaves * slots), jnp.int32),
            pltpu.SemaphoreType.DMA((2,)),
        ],
        compiler_params=pltpu.CompilerParams(vmem_limit_bytes=VMEM_BYTES),
        cost_estimate=pl.CostEstimate(flops=2**31, bytes_accessed=3 * 2**20, transcendentals=0),
        name="near_field",
    )(place, jnp.asarray(table), maps, jnp.asarray(weights, jnp.bfloat16), left, own, right)


def pack_kernel(points_ref, vectors_ref, lists_ref, out_ref):
    def chunk(i, _):
        cols = pl.ds(pl.multiple_of(i * 2048, 2048), 2048)
        centred = points_ref[:, cols] - 0.5
        hi = centred.astype(jnp.bfloat16).astype(jnp.float32)
        mid = centred - hi
        one = jnp.ones((1, 2048), jnp.float32)
        lists = jnp.where(i == 0, lists_ref[...], 0.0)
        rows = [vectors_ref[:, cols].astype(jnp.float32), hi, mid, one, lists]
        out_ref[:, cols] = jnp.concatenate(rows, axis=0).astype(jnp.bfloat16)
        return 0

    lax.fori_loop(0, points_ref.shape[1] // 2048, chunk, 0, unroll=2)


def pack_rows(points, vectors, lists):
    lists = jnp.pad(lists.astype(jnp.float32), (0, 2048 - lists.shape[0]))[None]
    vmem = pl.BlockSpec(memory_space=pltpu.VMEM)
    return pl.pallas_call(
        pack_kernel,
        out_shape=jax.ShapeDtypeStruct((16, points.shape[1]), jnp.bfloat16),
        in_specs=[vmem] * 3,
        out_specs=vmem,
        compiler_params=pltpu.CompilerParams(vmem_limit_bytes=VMEM_BYTES),
        cost_estimate=pl.CostEstimate(flops=2**20, bytes_accessed=2**20, transcendentals=0),
        name="pack_rows",
    )(points, vectors, lists)


def spread_map():
    r = lax.broadcasted_iota(jnp.int32, (64, 1024), 0)
    c = lax.broadcasted_iota(jnp.int32, (64, 1024), 1)
    wanted = ((c & 511) >> 4) * 2 + (c >> 9)
    return (r == wanted).astype(jnp.float32).astype(jnp.bfloat16)


def gather_map():
    c = lax.broadcasted_iota(jnp.int32, (1024, 64), 0)
    r = lax.broadcasted_iota(jnp.int32, (1024, 64), 1)
    wanted = ((c & 511) >> 4) * 2 + (c >> 9)
    return (r == wanted).astype(jnp.float32).astype(jnp.bfloat16)


def slot_mask(rows):
    r = lax.broadcasted_iota(jnp.int32, (rows, 1024), 0)
    c = lax.broadcasted_iota(jnp.int32, (rows, 1024), 1)
    return (r >> 3) == (c & 15)


def stacked(rows):
    return jnp.concatenate([rows[:, 128 * j : 128 * j + 128] for j in range(32)], axis=0)


def times_each(coef, blocks, spread, mask):
    wide = jnp.dot(coef, spread, preferred_element_type=jnp.float32)
    wide = jnp.where(mask, wide, 0.0).astype(jnp.bfloat16)
    first = jnp.dot(wide[:, :512], blocks, preferred_element_type=jnp.float32)
    second = jnp.dot(wide[:, 512:], blocks, preferred_element_type=jnp.float32)
    return first[:, :64] + second[:, 64:]


def pair_sum(product):
    rows = product.shape[0]
    pairs = product.reshape(rows // 16, 2, 8, product.shape[1])
    return (pairs[:, 0] + pairs[:, 1]).reshape(rows // 2, product.shape[1])


def doubled(parent):
    rows = parent.shape[0]
    tiles = parent.reshape(rows // 8, 1, 8, parent.shape[1])
    return jnp.concatenate([tiles, tiles], axis=1).reshape(rows * 2, parent.shape[1])


def back_wide(parent, blocks, mask):
    rows = parent.shape[0]
    none = jnp.zeros_like(parent)
    both = jnp.concatenate(
        [jnp.concatenate([parent, none], axis=1), jnp.concatenate([none, parent], axis=1)], axis=0
    ).astype(jnp.bfloat16)
    wide = lax.dot_general(both, blocks, (((1,), (1,)), ((), ())), preferred_element_type=jnp.float32)
    wide = jnp.concatenate([wide[:rows], wide[rows:]], axis=1)
    return jnp.where(mask, wide, 0.0).astype(jnp.bfloat16)


def back_each(parent, blocks, gather, mask):
    return jnp.dot(back_wide(parent, blocks, mask), gather, preferred_element_type=jnp.float32)


def last_rows(local_ref):
    rows = local_ref[local_ref.shape[0] - 16 :, :]
    keep = lax.broadcasted_iota(jnp.int32, rows.shape, 0) < 14
    return jnp.where(keep, rows.astype(jnp.float32), 0.0).astype(jnp.bfloat16)


def up_kernel(
    pack_ref,
    transfer_ref,
    couple_ref,
    last_ref,
    basis_hbm,
    local_hbm,
    coef_ref,
    top_ref,
    flat_ref,
    turn_ref,
    basis_ref,
    local_ref,
    sems,
):
    leaves = basis_ref.shape[0]

    def basis_copy(step):
        part = pl.ds(step * 8, 8)
        return pltpu.make_async_copy(basis_hbm.at[part], basis_ref.at[part], sems.at[step])

    local_copy = pltpu.make_async_copy(
        local_hbm.at[pl.ds(0, 2 * leaves - 16)], local_ref, sems.at[leaves // 8]
    )
    for step in range(leaves // 8):
        basis_copy(step).start()
    local_copy.start()
    spread, mask = spread_map(), slot_mask(128)

    def project(step, _):
        basis_copy(step).wait()
        for k in range(8):
            leaf = step * 8 + k
            block = pack_ref[:, pl.ds(pl.multiple_of(leaf * 256, 256), 256)]
            coef = lax.dot_general(
                block, basis_ref[leaf], (((1,), (1,)), ((), ())), preferred_element_type=jnp.float32
            )
            flat_ref[pl.ds(pl.multiple_of(leaf * 8, 8), 8), :] = coef[0:8]
        return 0

    lax.fori_loop(0, leaves // 8, project, 0)
    local_copy.wait()
    for v in range(8):
        turn_ref[pl.ds(v, 64, stride=8), :] = flat_ref[pl.ds(v, leaves, stride=8), :].T
    coef_ref[...] = turn_ref[...].astype(jnp.bfloat16)
    level = flat_ref[...].astype(jnp.bfloat16)
    width = leaves
    while width > 1:
        start = 2 * leaves - 2 * width
        if width >= 16:
            parts = []
            for g in range(width // 16):
                blocks = stacked(local_ref[start + 16 * g : start + 16 * g + 16, :])
                parts.append(pair_sum(times_each(level[128 * g : 128 * g + 128], blocks, spread, mask)))
            level = jnp.concatenate(parts, axis=0) if len(parts) > 1 else parts[0]
        else:
            first = start - (2 * leaves - 16)
            blocks = stacked(last_rows(last_ref))
            pieces = [level.astype(jnp.float32)]
            if first:
                pieces.insert(0, jnp.zeros((8 * first, 64), jnp.float32))
            rest = 16 - first - width
            if rest:
                pieces.append(jnp.zeros((8 * rest, 64), jnp.float32))
            padded = jnp.concatenate(pieces, axis=0).astype(jnp.bfloat16)
            product = times_each(padded, blocks, spread, mask)
            level = pair_sum(product[8 * first : 8 * (first + width)])
        level = level.astype(jnp.bfloat16)
        width //= 2
    mine = [transfer_ref[...]] + [couple_ref[s] for s in range(3)]
    mine = jnp.concatenate([x.astype(jnp.float32) for x in mine], axis=0).astype(jnp.bfloat16)
    level = jnp.concatenate([level, jnp.zeros_like(level)], axis=1)
    for device in range(top_ref.shape[0]):
        top_ref[device, :, 0:4096] = mine
        top_ref[device, :, 4096:4224] = level


def up_tree(devices, pack, transfer, couple, basis, local):
    leaves, rank, _ = basis.shape
    vmem = pl.BlockSpec(memory_space=pltpu.VMEM)
    return pl.pallas_call(
        up_kernel,
        out_shape=(
            jax.ShapeDtypeStruct((8 * rank, leaves), jnp.bfloat16),
            jax.ShapeDtypeStruct((devices, 8, rank * rank + 128), jnp.bfloat16),
        ),
        grid=(1,),
        in_specs=[
            vmem,
            vmem,
            vmem,
            pl.BlockSpec((16, rank * rank), lambda g: (2 * leaves // 16 - 1, 0)),
            pl.BlockSpec(memory_space=pltpu.HBM),
            pl.BlockSpec(memory_space=pltpu.HBM),
        ],
        out_specs=(vmem, vmem),
        scratch_shapes=[
            pltpu.VMEM((8 * leaves, rank), jnp.float32),
            pltpu.VMEM((8 * rank, leaves), jnp.float32),
            pltpu.VMEM(basis.shape, basis.dtype),
            pltpu.VMEM((2 * leaves - 16, rank * rank), jnp.bfloat16),
            pltpu.SemaphoreType.DMA((leaves // 8 + 1,)),
        ],
        compiler_params=pltpu.CompilerParams(vmem_limit_bytes=VMEM_BYTES),
        cost_estimate=pl.CostEstimate(flops=2 * 2**27, bytes_accessed=4 * 2**20, transcendentals=0),
        name="up_tree",
    )(pack, transfer, couple, local, basis, local)


def far_kernel(
    devices,
    place_ref,
    ids_ref,
    w0,
    w1,
    w2,
    w3,
    w4,
    last_ref,
    local_hbm,
    couple_hbm,
    upper_hbm,
    basis_hbm,
    out_ref,
    window_ref,
    vrows_ref,
    down_ref,
    couple_ref,
    upper_ref,
    basis_ref,
    local_ref,
    sems,
):
    leaves = basis_ref.shape[0]
    groups = leaves // 8
    f32, bf16 = jnp.float32, jnp.bfloat16
    upper_copy = pltpu.make_async_copy(upper_hbm, upper_ref, sems.at[0])
    basis_copy = pltpu.make_async_copy(basis_hbm, basis_ref, sems.at[1])
    local_copy = pltpu.make_async_copy(local_hbm.at[pl.ds(0, 2 * leaves - 16)], local_ref, sems.at[2])
    couple_copies = [
        pltpu.make_async_copy(
            couple_hbm.at[pl.ds(128 * g, 128)], couple_ref.at[pl.ds(128 * g, 128)], sems.at[3 + g]
        )
        for g in range(groups)
    ]
    couple_copies[0].start()
    upper_copy.start()
    for copy in couple_copies[1:]:
        copy.start()
    local_copy.start()
    basis_copy.start()
    for k, ref in enumerate((w0, w1, w2, w3, w4)):
        window_ref[:, 64 * k : 64 * k + 64] = ref[...]
    window_ref[:, 320:384] = jnp.zeros((512, 64), bf16)
    row = lax.broadcasted_iota(jnp.int32, (128, 128), 0)
    col = lax.broadcasted_iota(jnp.int32, (128, 128), 1)
    same = ((row >> 4) == (col >> 4)).astype(f32).astype(bf16)
    leaf_row = lax.broadcasted_iota(jnp.int32, (384, 128), 0)

    def coupling(g):
        couple_copies[g].wait()
        chosen = (leaf_row == ids_ref[g : g + 1, :]).astype(f32).astype(bf16)
        picked = jnp.dot(window_ref[...], chosen, preferred_element_type=f32).astype(bf16)
        summed = jnp.zeros((128, 128), f32)
        for j in range(0, 32, 2):
            left = jnp.concatenate(
                [jnp.concatenate([picked[16 * i : 16 * i + 16]] * 8, axis=0) * same for i in (j, j + 1)], axis=1
            )
            right = jnp.concatenate(
                [couple_ref[128 * g : 128 * g + 128, 128 * i : 128 * i + 128] for i in (j, j + 1)], axis=0
            )
            summed += jnp.dot(left, right, preferred_element_type=f32)
        parts = summed.reshape(8, 2, 8, 128)
        return parts[:, 0, :, :64].reshape(64, 64) + parts[:, 1, :, 64:].reshape(64, 64)

    def tree():
        me = place_ref[0]
        top_levels = devices.bit_length() - 1
        spread, gather, mask = spread_map(), gather_map(), slot_mask(128)
        heap = 2 * devices
        path_slots = 16
        couple_slots = -(-3 * top_levels // 16) * 16
        total = heap + path_slots + couple_slots
        q = lax.broadcasted_iota(jnp.int32, (total, 4 * heap), 0)
        c = lax.broadcasted_iota(jnp.int32, (total, 4 * heap), 1)
        k_v = q - heap
        node_v = jnp.where(q < heap, q, (devices + me) >> jnp.clip(k_v, 0, 31))
        want_v = 8 * (node_v >> 1) + (node_v & 1)
        q_c = q - heap - path_slots
        k_c = (q_c * 11) >> 5
        node_c = (devices + me) >> jnp.clip(k_c, 0, 31)
        want_c = 8 * (node_c >> 1) + 2 + 2 * (q_c - 3 * k_c) + (node_c & 1)
        wanted = jnp.where(q < heap + path_slots, want_v, want_c)
        chosen_rows = (c == wanted).astype(f32).astype(bf16)
        upper_copy.wait()
        for piece in range(8):
            cols = slice(512 * piece, 512 * piece + 512)
            vrows_ref[:, cols] = jnp.dot(chosen_rows, upper_ref[:, cols], preferred_element_type=f32).astype(bf16)
        yield
        top = [None] * top_levels
        level = upper_ref[:, 4096:4160]
        width = devices
        top[0] = level
        for k in range(1, top_levels):
            if width >= 16:
                parts = []
                for g in range(width // 16):
                    blocks = stacked(vrows_ref[width + 16 * g : width + 16 * g + 16, :])
                    parts.append(pair_sum(times_each(level[128 * g : 128 * g + 128], blocks, spread, mask)))
                level = jnp.concatenate(parts, axis=0) if len(parts) > 1 else parts[0]
            else:
                blocks = stacked(vrows_ref[0:16, :])
                pieces = [jnp.zeros((8 * width, 64), f32), level.astype(f32)]
                if 16 - 2 * width:
                    pieces.append(jnp.zeros((8 * (16 - 2 * width), 64), f32))
                padded = jnp.concatenate(pieces, axis=0).astype(bf16)
                product = times_each(padded, blocks, spread, mask)
                level = pair_sum(product[8 * width : 16 * width])
            level = level.astype(bf16)
            top[k] = level
            width //= 2
            yield
        whole = jnp.concatenate(
            [jnp.zeros((16, 64), f32)] + [top[k].astype(f32) for k in range(top_levels - 1, -1, -1)], axis=0
        ).astype(bf16)
        terms = []
        for t in range(couple_slots // 16):
            r = lax.broadcasted_iota(jnp.int32, (128, 8 * heap), 0)
            c = lax.broadcasted_iota(jnp.int32, (128, 8 * heap), 1)
            q = (r >> 3) + 16 * t
            k = (q * 11) >> 5
            s = q - 3 * k
            k = jnp.minimum(k, 31)
            node = me >> k
            odd = (node & 1) == 1
            offset = jnp.where(
                odd,
                jnp.where(s == 0, odd_offsets[0], jnp.where(s == 1, odd_offsets[1], odd_offsets[2])),
                jnp.where(s == 0, even_offsets[0], jnp.where(s == 1, even_offsets[1], even_offsets[2])),
            )
            partner = node + offset
            count = devices >> k
            live = (partner >= 0) & (partner < count) & (k < top_levels)
            want = jnp.where(live, (count + partner) * 8 + (r & 7), -1)
            sources = jnp.dot((c == want).astype(f32).astype(bf16), whole, preferred_element_type=f32).astype(bf16)
            blocks = stacked(vrows_ref[heap + path_slots + 16 * t : heap + path_slots + 16 * t + 16, :])
            product = times_each(sources, blocks, spread, mask)
            terms.extend(product[8 * i : 8 * i + 8] for i in range(16))
        yield
        path_blocks = stacked(vrows_ref[heap : heap + path_slots, :])
        lane = lax.broadcasted_iota(jnp.int32, (8, 1024), 1)
        parent = None
        for k in range(top_levels - 1, -1, -1):
            value = terms[3 * k] + terms[3 * k + 1] + terms[3 * k + 2]
            if parent is not None:
                value = value + back_each(parent, path_blocks, gather, (lane & 15) == k)
            parent = value.astype(bf16).astype(f32)
            yield
        local_copy.wait()
        width = 2
        while width <= leaves:
            start = 2 * leaves - 2 * width
            if width >= 16:
                parts = []
                for g in range(width // 16):
                    blocks = stacked(local_ref[start + 16 * g : start + 16 * g + 16, :])
                    pair = doubled(parent[64 * g : 64 * g + 64])
                    parts.append(back_wide(pair, blocks, mask))
                wide = jnp.concatenate(parts, axis=0) if len(parts) > 1 else parts[0]
                parent = jnp.dot(wide, gather, preferred_element_type=f32)
            else:
                first = start - (2 * leaves - 16)
                blocks = stacked(last_rows(last_ref))
                pieces = [doubled(parent)]
                if first:
                    pieces.insert(0, jnp.zeros((8 * first, 64), f32))
                rest = 16 - first - width
                if rest:
                    pieces.append(jnp.zeros((8 * rest, 64), f32))
                parent = back_each(jnp.concatenate(pieces, axis=0), blocks, gather, mask)
                parent = parent[8 * first : 8 * (first + width)]
            width *= 2
            if width <= leaves:
                yield
        down_ref[...] = parent

    steps = tree()
    sums = []
    for g in range(groups):
        sums.append(coupling(g))
        for _ in range(2):
            next(steps, None)
    for _ in steps:
        pass
    for g in range(groups):
        down_ref[64 * g : 64 * g + 64, :] += sums[g]
    basis_copy.wait()

    def expand(step, _):
        for k in range(8):
            leaf = step * 8 + k
            mine = down_ref[pl.ds(pl.multiple_of(leaf * 8, 8), 8), :].astype(bf16)
            cols = pl.ds(pl.multiple_of(leaf * 256, 256), 256)
            out_ref[:, cols] = jnp.dot(mine, basis_ref[leaf], preferred_element_type=f32)
        return 0

    lax.fori_loop(0, leaves // 8, expand, 0)


def far_field(devices, place, ids, window, couple, upper, local, basis):
    leaves, rank, leaf_size = basis.shape
    top_levels = devices.bit_length() - 1
    rows = 2 * devices + 16 + -(-3 * top_levels // 16) * 16
    vmem = pl.BlockSpec(memory_space=pltpu.VMEM)
    return pl.pallas_call(
        lambda *refs: far_kernel(devices, *refs),
        grid=(1,),
        out_shape=jax.ShapeDtypeStruct((8, leaves * leaf_size), jnp.float32),
        in_specs=[pl.BlockSpec(memory_space=pltpu.SMEM)]
        + [vmem] * 6
        + [pl.BlockSpec((16, rank * rank), lambda g: (2 * leaves // 16 - 1, 0))]
        + [pl.BlockSpec(memory_space=pltpu.HBM)] * 4,
        out_specs=vmem,
        scratch_shapes=[
            pltpu.VMEM((8 * rank, 384), jnp.bfloat16),
            pltpu.VMEM((rows, 4096), jnp.bfloat16),
            pltpu.VMEM((8 * leaves, rank), jnp.float32),
            pltpu.VMEM(couple.shape, couple.dtype),
            pltpu.VMEM(upper.shape, upper.dtype),
            pltpu.VMEM(basis.shape, basis.dtype),
            pltpu.VMEM((2 * leaves - 16, rank * rank), jnp.bfloat16),
            pltpu.SemaphoreType.DMA((3 + leaves // 8,)),
        ],
        compiler_params=pltpu.CompilerParams(
            vmem_limit_bytes=VMEM_BYTES, dimension_semantics=("arbitrary",)
        ),
        cost_estimate=pl.CostEstimate(flops=2 * 2**28, bytes_accessed=16 * 2**20, transcendentals=0),
        name="far_field",
    )(place, ids, *window, local, local, couple, upper, basis)


def shards(
    points,
    vectors,
    near_list,
    near_count,
    couple_list,
    leaf_basis,
    local_transfer,
    couple_block,
    upper_transfer,
    upper_couple,
):
    devices = lax.axis_size(AXES)
    my_index = lax.axis_index(AXES).astype(jnp.int32)
    leaves, rank, leaf_size = leaf_basis.shape
    couple_slots = couple_list.shape[1]

    local_near = near_list - (my_index - 1) * leaves
    slot = jnp.arange(near_list.shape[1], dtype=jnp.int32)[None, :]
    lists = jnp.where(slot < near_count[:, None], local_near + 1, 0).reshape(-1)
    own = pack_rows(points, vectors, lists)
    place = my_index.reshape(1)
    left = from_behind(own, 1)
    right = from_behind(own, -1)
    local = local_transfer[0]
    coef, upper = up_tree(devices, own, upper_transfer, upper_couple.transpose(1, 0, 2), leaf_basis, local)
    window = [from_behind(coef, d) if d else coef for d in range(REACH, -REACH - 1, -1)]
    upper, left, right = lax.optimization_barrier((upper, left, right))
    upper = lax.all_to_all(upper, AXES, 0, 0, tiled=True)

    near = near_field(devices, place, leaves, near_list.shape[1], left, own, right)
    for_left, near, for_right, upper, window = lax.optimization_barrier((*near, upper, window))
    from_right = from_behind(for_left, -1)
    from_left = from_behind(for_right, 1)

    ids = (couple_list - (my_index - REACH) * leaves).reshape(leaves // 8, 8 * couple_slots)
    couple = couple_block.reshape(leaves * couple_slots, rank * rank)
    far = far_field(
        devices, place, ids, window, couple, upper.reshape(devices * 8, -1), local, leaf_basis
    )
    return far + near + (from_left + from_right)


def solution(mesh):
    placed = (
        P(None, AXES),
        P(None, AXES),
        P(AXES, None),
        P(AXES),
        P(AXES, None),
        P(AXES, None, None),
        P(AXES, None, None),
        P(AXES, None, None),
        P(AXES, None),
        P(AXES, None, None),
    )
    return jax.shard_map(shards, mesh=mesh, in_specs=placed, out_specs=P(None, AXES), check_vma=False)
```

```python
import math

import jax
import jax.numpy as jnp
import numpy as np
from jax import lax
from jax.experimental import pallas as pl
from jax.experimental.pallas import tpu as pltpu
from jax.sharding import PartitionSpec as P

REACH = 2
AXES = ("sect", "dev")
UNROLL = 8
VMEM_BYTES = 58 * 1024 * 1024

soft_sq = 0.0025
even_offsets = (-2, 2, 3)
odd_offsets = (-3, -2, 2)


def from_behind(block, distance):
    devices = range(lax.axis_size(AXES))
    route = [(i - distance, i) for i in devices if i - distance in devices]
    return lax.ppermute(block, AXES, route)


def feature_maps():
    source = np.zeros((32, 16), np.float32)
    target = np.zeros((32, 16), np.float32)
    coords = np.zeros((8, 16), np.float32)
    for c in range(3):
        hi, mid = 8 + c, 11 + c
        source[c, hi] = source[3 + c, hi] = 1.0
        source[6 + c, mid] = source[9 + c, mid] = 1.0
        target[c, hi] = target[6 + c, hi] = -2.0
        target[3 + c, mid] = target[9 + c, mid] = -2.0
        coords[c, hi] = coords[c, mid] = 1.0
    source[15:18, 14] = 1.0
    target[12:15, 14] = 1.0
    return source, coords, target


def split3(x):
    a = x.astype(jnp.bfloat16).astype(jnp.float32)
    b = (x - a).astype(jnp.bfloat16).astype(jnp.float32)
    c = (x - a - b).astype(jnp.bfloat16).astype(jnp.float32)
    return a, b, c


def flow(a, b, only):
    gap = a - b
    return jnp.where((a > 0) & (b > 0) & (gap > 24), (gap * jnp.where(only, 128, 85)) >> 8, 0)


def near_kernel(
    devices,
    place_ref,
    low_bit,
    maps_ref,
    weights_ref,
    left_ref,
    own_ref,
    right_ref,
    left_out,
    own_out,
    right_out,
    s_own,
    s_side,
    t_ref,
    v_own,
    v_side,
    g_even,
    g_odd,
    sum_ref,
    masks_v,
    ids_v,
    masks,
    ids,
    sems,
):
    leaves = own_ref.shape[1] // 256
    slots = weights_ref.shape[0] // leaves
    kernel_scale = 1.0 / math.sqrt(256 * (slots + 1))
    row = lax.broadcasted_iota(jnp.int32, (8, 2048), 0)
    zero = jnp.int32(0)
    f32 = jnp.float32

    def listed(ref):
        return ref[8:16, 0 : leaves * slots].astype(f32)[7:8]

    def band(x, k):
        return jnp.where((x > leaves * k) & (x <= leaves * (k + 1)), 1.0, 0.0)

    mine, theirs_l, theirs_r = listed(own_ref), listed(left_ref), listed(right_ref)
    flags = [band(mine, 1), band(mine, 0), band(mine, 2), band(theirs_l, 2), band(theirs_r, 0)]
    flags += [jnp.where(x > 0.0, 1.0, 0.0) for x in (mine, theirs_l, theirs_r)]
    flags = jnp.concatenate(flags, axis=0).astype(jnp.bfloat16)
    masks_v[...] = jnp.dot(flags, weights_ref[...], preferred_element_type=f32).astype(jnp.int32)
    places = [mine - (leaves + 1.0), theirs_l - (2 * leaves + 1.0), theirs_r - 1.0]
    places += [jnp.zeros((5, leaves * slots), f32)]
    ids_v[...] = jnp.concatenate(places, axis=0).astype(jnp.int32)
    masks_copy = pltpu.make_async_copy(masks_v, masks, sems.at[0])
    ids_copy = pltpu.make_async_copy(ids_v, ids, sems.at[1])
    masks_copy.start()
    ids_copy.start()

    def put_source(ref, chunk, s_ref, v_ref, leaf, target):
        block = ref[:, pl.ds(pl.multiple_of(chunk * 2048, 2048), 2048)]
        wide = jnp.dot(maps_ref[...], block, preferred_element_type=f32)
        coord = wide[32:40]
        norm = jnp.sum(coord * coord, axis=0, keepdims=True)
        a, b, c = split3(norm)
        mixed = jnp.where(row == 7, 1.0, wide[8:16])
        mixed = jnp.where(row == 4, a, jnp.where(row == 5, b, jnp.where(row == 6, c, mixed)))
        rows = jnp.concatenate([wide[0:8], mixed, wide[16:32]], axis=0).astype(jnp.bfloat16)
        for half in range(2):
            quad = [rows[:, 256 * k : 256 * k + 256] for k in range(4 * half, 4 * half + 4)]
            turned = jnp.concatenate(quad, axis=0).T
            for k in range(4):
                s_ref[leaf + 4 * half + k] = turned[:, 32 * k : 32 * k + 32]
        for k in range(8):
            v_ref[leaf + k] = block[:, 256 * k : 256 * k + 256]
        a, b, c = split3(norm + soft_sq)
        first = jnp.where(row == 7, a, wide[48:56])
        second = jnp.where(row == 0, b, jnp.where(row == 1, c, wide[56:64]))
        rows = jnp.concatenate([wide[40:48], first, second, wide[64:72]], axis=0).astype(jnp.bfloat16)
        for k in range(8):
            t_ref[target + k] = rows[:, 256 * k : 256 * k + 256]

    def build_own(chunk, _):
        put_source(own_ref, chunk, s_own, v_own, chunk * 8, chunk * 8)
        return 0

    lax.fori_loop(0, leaves // 8, build_own, 0, unroll=4)
    v_own[leaves] = jnp.zeros((16, 256), jnp.bfloat16)
    v_side[2 * leaves] = jnp.zeros((16, 256), jnp.bfloat16)
    sum_ref[...] = jnp.zeros_like(sum_ref)
    masks_copy.wait()
    ids_copy.wait()

    def pairs(k):
        found = masks[k, 2 * leaves]
        return jnp.where(found > 0, found + leaves, 0)

    here, at_left, at_right = pairs(5), pairs(6), pairs(7)
    me = place_ref[0]

    def whole_rows(k, allowed):
        def fits(carry):
            t, total = carry
            return (t < leaves) & (total + masks[k, leaves + jnp.minimum(t, leaves - 1)] <= allowed)

        def step(carry):
            t, total = carry
            return t + 1, total + masks[k, leaves + t]

        rows, _ = lax.while_loop(fits, step, (jnp.where(allowed > 0, 0, leaves).astype(jnp.int32), zero))
        return jnp.where(allowed > 0, rows, 0)

    give_left = whole_rows(1, flow(here, at_left, at_right == 0))
    give_right = whole_rows(2, flow(here, at_right, at_left == 0))
    take_left = whole_rows(3, flow(at_left, here, me == 1))
    take_right = whole_rows(4, flow(at_right, here, me == devices - 2))

    def mask_of(at, own):
        if own:
            at = jnp.minimum(at, 3 * leaves - 1)
            k = jnp.where(at < leaves, 0, jnp.where(at < 2 * leaves, 3, 4))
            return masks[k, at & (leaves - 1)] | jnp.where(at < leaves, 1 << slots, 0)
        at = jnp.minimum(at, leaves - 1)
        return jnp.where(at < give_left, 0, masks[1, at]) | jnp.where(at < give_right, 0, masks[2, at])

    def after_row(at, own):
        if own:
            return jnp.where(at + 1 == leaves + take_left, 2 * leaves, at + 1)
        return at + 1

    def add_held(held, g_in, v_ref):
        return [jnp.dot(v_ref[held[u][0]], g_in[u], preferred_element_type=f32) for u in range(UNROLL)]

    def put_held(held, updates):
        for u in range(UNROLL):
            sum_ref[held[u][1]] += updates[u][0:8]

    def half(state, held, g_in, g_out, own, end):
        at, mask = state
        fresh = []
        s_ref, v_ref = (s_own, v_own) if own else (s_side, v_side)
        idle = leaves if own else 2 * leaves
        updates = add_held(held, g_in, v_ref)
        for u in range(UNROLL):
            active = at < end
            target = jnp.where(active, at, 0)
            low = mask & -mask
            slot = low_bit[lax.shift_right_logical(low * 0x077CB531, 27)]
            place = ids[target >> (leaves.bit_length() - 1), (target & (leaves - 1)) * slots + jnp.minimum(slot, slots - 1)]
            if own:
                source = jnp.where(slot == slots, target, place)
            else:
                source = jnp.where(place < 0, place + leaves, place)
            used = active & (low != 0)
            source = jnp.where(used, source, 0)
            fresh.append((jnp.where(used, source, idle), target))
            dist = jnp.dot(s_ref[source], t_ref[target], preferred_element_type=f32)
            g_out[u] = lax.rsqrt(dist.astype(jnp.bfloat16))
            rest = mask ^ low
            done = active & (rest == 0)
            following = after_row(at, own)
            mask = jnp.where(done, mask_of(following, own), jnp.where(active, rest, mask))
            at = jnp.where(done, following, at)
        put_held(held, updates)
        return (at, mask), tuple(fresh)

    def both(state, held, own, end):
        state, held = half(state, held, g_even, g_odd, own, end)
        return half(state, held, g_odd, g_even, own, end)

    def nothing(own):
        idle = leaves if own else 2 * leaves
        return tuple((jnp.int32(idle), zero) for _ in range(UNROLL))

    def first_bodies(chunk, carry):
        carry = both(*carry, True, leaves)
        put_source(left_ref, chunk, s_side, v_side, chunk * 8, leaves + chunk * 8)
        put_source(right_ref, chunk, s_side, v_side, leaves + chunk * 8, 2 * leaves + chunk * 8)
        return carry

    def run(own, end, state, held):
        def more(carry):
            return carry[0][0] < end

        state, held = lax.while_loop(more, lambda carry: both(*carry, own, end), (state, held))
        put_held(held, add_held(held, g_even, v_own if own else v_side))

    g_even[...] = jnp.zeros_like(g_even)
    state, held = lax.fori_loop(0, leaves // 8, first_bodies, ((zero, mask_of(zero, True)), nothing(True)))
    run(True, 2 * leaves + take_right, state, held)
    run(False, leaves, (zero, mask_of(zero, False)), nothing(False))

    def finish(chunk, _):
        for k in range(8):
            leaf = chunk * 8 + k
            cols = pl.ds(pl.multiple_of(leaf * 256, 256), 256)
            for side, ref in enumerate((own_out, left_out, right_out)):
                ref[:, cols] = sum_ref[side * leaves + leaf] * kernel_scale
        return 0

    lax.fori_loop(0, leaves // 8, finish, 0)


def near_field(devices, place, leaves, slots, left, own, right):
    points = own.shape[1]
    maps = jnp.asarray(np.concatenate(feature_maps(), axis=0), jnp.bfloat16)
    table = np.zeros((32,), np.int32)
    for bit in range(32):
        table[((0x077CB531 << bit) & 0xFFFFFFFF) >> 27] = bit
    weights = np.zeros((leaves * slots, 256), np.float32)
    for t in range(leaves):
        for k in range(slots):
            weights[t * slots + k, t] = 2.0**k
            weights[t * slots + k, leaves + t] = 1.0
    weights[:, 2 * leaves] = 1.0
    smem = pl.BlockSpec(memory_space=pltpu.SMEM)
    vmem = pl.BlockSpec(memory_space=pltpu.VMEM)
    return pl.pallas_call(
        lambda *refs: near_kernel(devices, *refs),
        out_shape=(jax.ShapeDtypeStruct((8, points), jnp.float32),) * 3,
        in_specs=[smem] * 2 + [vmem] * 5,
        out_specs=(vmem,) * 3,
        scratch_shapes=[
            pltpu.VMEM((leaves, 256, 32), jnp.bfloat16),
            pltpu.VMEM((2 * leaves, 256, 32), jnp.bfloat16),
            pltpu.VMEM((3 * leaves, 32, 256), jnp.bfloat16),
            pltpu.VMEM((leaves + 1, 16, 256), jnp.bfloat16),
            pltpu.VMEM((2 * leaves + 1, 16, 256), jnp.bfloat16),
            pltpu.VMEM((UNROLL, 256, 256), jnp.bfloat16),
            pltpu.VMEM((UNROLL, 256, 256), jnp.bfloat16),
            pltpu.VMEM((3 * leaves, 8, 256), jnp.float32),
            pltpu.VMEM((8, 256), jnp.int32),
            pltpu.VMEM((8, leaves * slots), jnp.int32),
            pltpu.SMEM((8, 256), jnp.int32),
            pltpu.SMEM((8, leaves * slots), jnp.int32),
            pltpu.SemaphoreType.DMA((2,)),
        ],
        compiler_params=pltpu.CompilerParams(vmem_limit_bytes=VMEM_BYTES),
        cost_estimate=pl.CostEstimate(flops=2**31, bytes_accessed=3 * 2**20, transcendentals=0),
        name="near_field",
    )(place, jnp.asarray(table), maps, jnp.asarray(weights, jnp.bfloat16), left, own, right)


def pack_kernel(points_ref, vectors_ref, lists_ref, out_ref):
    rest = jnp.zeros((1, 2048 - lists_ref.shape[1]), jnp.float32)

    def chunk(i, _):
        cols = pl.ds(pl.multiple_of(i * 2048, 2048), 2048)
        centred = points_ref[:, cols] - 0.5
        hi = centred.astype(jnp.bfloat16).astype(jnp.float32)
        mid = centred - hi
        one = jnp.ones((1, 2048), jnp.float32)
        lists = jnp.where(i == 0, jnp.concatenate([lists_ref[...], rest], axis=1), 0.0)
        rows = [vectors_ref[:, cols].astype(jnp.float32), hi, mid, one, lists]
        out_ref[:, cols] = jnp.concatenate(rows, axis=0).astype(jnp.bfloat16)
        return 0

    lax.fori_loop(0, points_ref.shape[1] // 2048, chunk, 0, unroll=2)


def pack_rows(points, vectors, lists):
    lists = lists.astype(jnp.float32)[None]
    vmem = pl.BlockSpec(memory_space=pltpu.VMEM)
    return pl.pallas_call(
        pack_kernel,
        out_shape=jax.ShapeDtypeStruct((16, points.shape[1]), jnp.bfloat16),
        in_specs=[vmem] * 3,
        out_specs=vmem,
        compiler_params=pltpu.CompilerParams(vmem_limit_bytes=VMEM_BYTES),
        cost_estimate=pl.CostEstimate(flops=2**20, bytes_accessed=2**20, transcendentals=0),
        name="pack_rows",
    )(points, vectors, lists)


def spread_map():
    r = lax.broadcasted_iota(jnp.int32, (64, 1024), 0)
    c = lax.broadcasted_iota(jnp.int32, (64, 1024), 1)
    wanted = ((c & 511) >> 4) * 2 + (c >> 9)
    return (r == wanted).astype(jnp.float32).astype(jnp.bfloat16)


def gather_map():
    c = lax.broadcasted_iota(jnp.int32, (1024, 64), 0)
    r = lax.broadcasted_iota(jnp.int32, (1024, 64), 1)
    wanted = ((c & 511) >> 4) * 2 + (c >> 9)
    return (r == wanted).astype(jnp.float32).astype(jnp.bfloat16)


def slot_mask(rows):
    r = lax.broadcasted_iota(jnp.int32, (rows, 1024), 0)
    c = lax.broadcasted_iota(jnp.int32, (rows, 1024), 1)
    return (r >> 3) == (c & 15)


def stacked(rows):
    return jnp.concatenate([rows[:, 128 * j : 128 * j + 128] for j in range(32)], axis=0)


def times_each(coef, blocks, spread, mask):
    wide = jnp.dot(coef, spread, preferred_element_type=jnp.float32)
    wide = jnp.where(mask, wide, 0.0).astype(jnp.bfloat16)
    first = jnp.dot(wide[:, :512], blocks, preferred_element_type=jnp.float32)
    second = jnp.dot(wide[:, 512:], blocks, preferred_element_type=jnp.float32)
    return first[:, :64] + second[:, 64:]


def pair_sum(product):
    rows = product.shape[0]
    pairs = product.reshape(rows // 16, 2, 8, product.shape[1])
    return (pairs[:, 0] + pairs[:, 1]).reshape(rows // 2, product.shape[1])


def doubled(parent):
    rows = parent.shape[0]
    tiles = parent.reshape(rows // 8, 1, 8, parent.shape[1])
    return jnp.concatenate([tiles, tiles], axis=1).reshape(rows * 2, parent.shape[1])


def back_wide(parent, blocks, mask):
    rows = parent.shape[0]
    none = jnp.zeros_like(parent)
    both = jnp.concatenate(
        [jnp.concatenate([parent, none], axis=1), jnp.concatenate([none, parent], axis=1)], axis=0
    ).astype(jnp.bfloat16)
    wide = lax.dot_general(both, blocks, (((1,), (1,)), ((), ())), preferred_element_type=jnp.float32)
    wide = jnp.concatenate([wide[:rows], wide[rows:]], axis=1)
    return jnp.where(mask, wide, 0.0).astype(jnp.bfloat16)


def back_each(parent, blocks, gather, mask):
    return jnp.dot(back_wide(parent, blocks, mask), gather, preferred_element_type=jnp.float32)


def last_rows(local_ref):
    rows = local_ref[local_ref.shape[0] - 16 :, :]
    keep = lax.broadcasted_iota(jnp.int32, rows.shape, 0) < 14
    return jnp.where(keep, rows.astype(jnp.float32), 0.0).astype(jnp.bfloat16)


def up_kernel(
    pack_ref,
    transfer_ref,
    couple_ref,
    last_ref,
    basis_hbm,
    local_hbm,
    coef_ref,
    top_ref,
    flat_ref,
    turn_ref,
    basis_ref,
    local_ref,
    sems,
):
    leaves = basis_ref.shape[0]

    def basis_copy(step):
        part = pl.ds(step * 8, 8)
        return pltpu.make_async_copy(basis_hbm.at[part], basis_ref.at[part], sems.at[step])

    local_copy = pltpu.make_async_copy(
        local_hbm.at[pl.ds(0, 2 * leaves - 16)], local_ref, sems.at[leaves // 8]
    )
    for step in range(leaves // 8):
        basis_copy(step).start()
    local_copy.start()
    spread, mask = spread_map(), slot_mask(128)

    def project(step, _):
        basis_copy(step).wait()
        for k in range(8):
            leaf = step * 8 + k
            block = pack_ref[:, pl.ds(pl.multiple_of(leaf * 256, 256), 256)]
            coef = lax.dot_general(
                block, basis_ref[leaf], (((1,), (1,)), ((), ())), preferred_element_type=jnp.float32
            )
            flat_ref[pl.ds(pl.multiple_of(leaf * 8, 8), 8), :] = coef[0:8]
        return 0

    lax.fori_loop(0, leaves // 8, project, 0, unroll=4)
    local_copy.wait()
    for v in range(8):
        turn_ref[pl.ds(v, 64, stride=8), :] = flat_ref[pl.ds(v, leaves, stride=8), :].T
    coef_ref[...] = turn_ref[...].astype(jnp.bfloat16)
    level = flat_ref[...].astype(jnp.bfloat16)
    width = leaves
    while width > 1:
        start = 2 * leaves - 2 * width
        if width >= 16:
            parts = []
            for g in range(width // 16):
                blocks = stacked(local_ref[start + 16 * g : start + 16 * g + 16, :])
                parts.append(pair_sum(times_each(level[128 * g : 128 * g + 128], blocks, spread, mask)))
            level = jnp.concatenate(parts, axis=0) if len(parts) > 1 else parts[0]
        else:
            first = start - (2 * leaves - 16)
            blocks = stacked(last_rows(last_ref))
            pieces = [level.astype(jnp.float32)]
            if first:
                pieces.insert(0, jnp.zeros((8 * first, 64), jnp.float32))
            rest = 16 - first - width
            if rest:
                pieces.append(jnp.zeros((8 * rest, 64), jnp.float32))
            padded = jnp.concatenate(pieces, axis=0).astype(jnp.bfloat16)
            product = times_each(padded, blocks, spread, mask)
            level = pair_sum(product[8 * first : 8 * (first + width)])
        level = level.astype(jnp.bfloat16)
        width //= 2
    mine = [transfer_ref[...]] + [couple_ref[s] for s in range(3)]
    mine = jnp.concatenate([x.astype(jnp.float32) for x in mine], axis=0).astype(jnp.bfloat16)
    level = jnp.concatenate([level, jnp.zeros_like(level)], axis=1)
    for device in range(top_ref.shape[0]):
        top_ref[device, :, 0:4096] = mine
        top_ref[device, :, 4096:4224] = level


def up_tree(devices, pack, transfer, couple, basis, local):
    leaves, rank, _ = basis.shape
    vmem = pl.BlockSpec(memory_space=pltpu.VMEM)
    return pl.pallas_call(
        up_kernel,
        out_shape=(
            jax.ShapeDtypeStruct((8 * rank, leaves), jnp.bfloat16),
            jax.ShapeDtypeStruct((devices, 8, rank * rank + 128), jnp.bfloat16),
        ),
        grid=(1,),
        in_specs=[
            vmem,
            vmem,
            vmem,
            pl.BlockSpec((16, rank * rank), lambda g: (2 * leaves // 16 - 1, 0)),
            pl.BlockSpec(memory_space=pltpu.HBM),
            pl.BlockSpec(memory_space=pltpu.HBM),
        ],
        out_specs=(vmem, vmem),
        scratch_shapes=[
            pltpu.VMEM((8 * leaves, rank), jnp.float32),
            pltpu.VMEM((8 * rank, leaves), jnp.float32),
            pltpu.VMEM(basis.shape, basis.dtype),
            pltpu.VMEM((2 * leaves - 16, rank * rank), jnp.bfloat16),
            pltpu.SemaphoreType.DMA((leaves // 8 + 1,)),
        ],
        compiler_params=pltpu.CompilerParams(vmem_limit_bytes=VMEM_BYTES),
        cost_estimate=pl.CostEstimate(flops=2 * 2**27, bytes_accessed=4 * 2**20, transcendentals=0),
        name="up_tree",
    )(pack, transfer, couple, local, basis, local)


def far_kernel(
    devices,
    place_ref,
    ids_ref,
    w0,
    w1,
    w2,
    w3,
    w4,
    last_ref,
    local_hbm,
    couple_hbm,
    upper_hbm,
    basis_hbm,
    out_ref,
    window_ref,
    vrows_ref,
    down_ref,
    couple_ref,
    upper_ref,
    basis_ref,
    local_ref,
    sems,
):
    leaves = basis_ref.shape[0]
    groups = leaves // 8
    f32, bf16 = jnp.float32, jnp.bfloat16
    upper_copy = pltpu.make_async_copy(upper_hbm, upper_ref, sems.at[0])
    basis_copy = pltpu.make_async_copy(basis_hbm, basis_ref, sems.at[1])
    local_copy = pltpu.make_async_copy(local_hbm.at[pl.ds(0, 2 * leaves - 16)], local_ref, sems.at[2])
    couple_copies = [
        pltpu.make_async_copy(
            couple_hbm.at[pl.ds(128 * g, 128)], couple_ref.at[pl.ds(128 * g, 128)], sems.at[3 + g]
        )
        for g in range(groups)
    ]
    couple_copies[0].start()
    upper_copy.start()
    for copy in couple_copies[1:]:
        copy.start()
    local_copy.start()
    basis_copy.start()
    for k, ref in enumerate((w0, w1, w2, w3, w4)):
        window_ref[:, 64 * k : 64 * k + 64] = ref[...]
    window_ref[:, 320:384] = jnp.zeros((512, 64), bf16)
    row = lax.broadcasted_iota(jnp.int32, (128, 128), 0)
    col = lax.broadcasted_iota(jnp.int32, (128, 128), 1)
    same = ((row >> 4) == (col >> 4)).astype(f32).astype(bf16)
    leaf_row = lax.broadcasted_iota(jnp.int32, (384, 128), 0)

    def coupling(g):
        couple_copies[g].wait()
        chosen = (leaf_row == ids_ref[g : g + 1, :]).astype(f32).astype(bf16)
        picked = jnp.dot(window_ref[...], chosen, preferred_element_type=f32).astype(bf16)
        summed = jnp.zeros((128, 128), f32)
        for j in range(0, 32, 2):
            left = jnp.concatenate(
                [jnp.concatenate([picked[16 * i : 16 * i + 16]] * 8, axis=0) * same for i in (j, j + 1)], axis=1
            )
            right = jnp.concatenate(
                [couple_ref[128 * g : 128 * g + 128, 128 * i : 128 * i + 128] for i in (j, j + 1)], axis=0
            )
            summed += jnp.dot(left, right, preferred_element_type=f32)
        parts = summed.reshape(8, 2, 8, 128)
        return parts[:, 0, :, :64].reshape(64, 64) + parts[:, 1, :, 64:].reshape(64, 64)

    def tree():
        me = place_ref[0]
        top_levels = devices.bit_length() - 1
        spread, gather, mask = spread_map(), gather_map(), slot_mask(128)
        heap = 2 * devices
        path_slots = 16
        couple_slots = -(-3 * top_levels // 16) * 16
        total = heap + path_slots + couple_slots
        q = lax.broadcasted_iota(jnp.int32, (total, 4 * heap), 0)
        c = lax.broadcasted_iota(jnp.int32, (total, 4 * heap), 1)
        k_v = q - heap
        node_v = jnp.where(q < heap, q, (devices + me) >> jnp.clip(k_v, 0, 31))
        want_v = 8 * (node_v >> 1) + (node_v & 1)
        q_c = q - heap - path_slots
        k_c = (q_c * 11) >> 5
        node_c = (devices + me) >> jnp.clip(k_c, 0, 31)
        want_c = 8 * (node_c >> 1) + 2 + 2 * (q_c - 3 * k_c) + (node_c & 1)
        wanted = jnp.where(q < heap + path_slots, want_v, want_c)
        chosen_rows = (c == wanted).astype(f32).astype(bf16)
        upper_copy.wait()
        for piece in range(8):
            cols = slice(512 * piece, 512 * piece + 512)
            vrows_ref[:, cols] = jnp.dot(chosen_rows, upper_ref[:, cols], preferred_element_type=f32).astype(bf16)
        yield
        top = [None] * top_levels
        level = upper_ref[:, 4096:4160]
        width = devices
        top[0] = level
        for k in range(1, top_levels):
            if width >= 16:
                parts = []
                for g in range(width // 16):
                    blocks = stacked(vrows_ref[width + 16 * g : width + 16 * g + 16, :])
                    parts.append(pair_sum(times_each(level[128 * g : 128 * g + 128], blocks, spread, mask)))
                level = jnp.concatenate(parts, axis=0) if len(parts) > 1 else parts[0]
            else:
                blocks = stacked(vrows_ref[0:16, :])
                pieces = [jnp.zeros((8 * width, 64), f32), level.astype(f32)]
                if 16 - 2 * width:
                    pieces.append(jnp.zeros((8 * (16 - 2 * width), 64), f32))
                padded = jnp.concatenate(pieces, axis=0).astype(bf16)
                product = times_each(padded, blocks, spread, mask)
                level = pair_sum(product[8 * width : 16 * width])
            level = level.astype(bf16)
            top[k] = level
            width //= 2
            yield
        whole = jnp.concatenate(
            [jnp.zeros((16, 64), f32)] + [top[k].astype(f32) for k in range(top_levels - 1, -1, -1)], axis=0
        ).astype(bf16)
        terms = []
        for t in range(couple_slots // 16):
            r = lax.broadcasted_iota(jnp.int32, (128, 8 * heap), 0)
            c = lax.broadcasted_iota(jnp.int32, (128, 8 * heap), 1)
            q = (r >> 3) + 16 * t
            k = (q * 11) >> 5
            s = q - 3 * k
            k = jnp.minimum(k, 31)
            node = me >> k
            odd = (node & 1) == 1
            offset = jnp.where(
                odd,
                jnp.where(s == 0, odd_offsets[0], jnp.where(s == 1, odd_offsets[1], odd_offsets[2])),
                jnp.where(s == 0, even_offsets[0], jnp.where(s == 1, even_offsets[1], even_offsets[2])),
            )
            partner = node + offset
            count = devices >> k
            live = (partner >= 0) & (partner < count) & (k < top_levels)
            want = jnp.where(live, (count + partner) * 8 + (r & 7), -1)
            sources = jnp.dot((c == want).astype(f32).astype(bf16), whole, preferred_element_type=f32).astype(bf16)
            blocks = stacked(vrows_ref[heap + path_slots + 16 * t : heap + path_slots + 16 * t + 16, :])
            product = times_each(sources, blocks, spread, mask)
            terms.extend(product[8 * i : 8 * i + 8] for i in range(16))
        yield
        path_blocks = stacked(vrows_ref[heap : heap + path_slots, :])
        lane = lax.broadcasted_iota(jnp.int32, (8, 1024), 1)
        parent = None
        for k in range(top_levels - 1, -1, -1):
            value = terms[3 * k] + terms[3 * k + 1] + terms[3 * k + 2]
            if parent is not None:
                value = value + back_each(parent, path_blocks, gather, (lane & 15) == k)
            parent = value.astype(bf16).astype(f32)
            yield
        local_copy.wait()
        width = 2
        while width <= leaves:
            start = 2 * leaves - 2 * width
            if width >= 16:
                parts = []
                for g in range(width // 16):
                    blocks = stacked(local_ref[start + 16 * g : start + 16 * g + 16, :])
                    pair = doubled(parent[64 * g : 64 * g + 64])
                    parts.append(back_wide(pair, blocks, mask))
                wide = jnp.concatenate(parts, axis=0) if len(parts) > 1 else parts[0]
                parent = jnp.dot(wide, gather, preferred_element_type=f32)
            else:
                first = start - (2 * leaves - 16)
                blocks = stacked(last_rows(last_ref))
                pieces = [doubled(parent)]
                if first:
                    pieces.insert(0, jnp.zeros((8 * first, 64), f32))
                rest = 16 - first - width
                if rest:
                    pieces.append(jnp.zeros((8 * rest, 64), f32))
                parent = back_each(jnp.concatenate(pieces, axis=0), blocks, gather, mask)
                parent = parent[8 * first : 8 * (first + width)]
            width *= 2
            if width <= leaves:
                yield
        down_ref[...] = parent

    steps = tree()
    sums = []
    for g in range(groups):
        sums.append(coupling(g))
        for _ in range(2):
            next(steps, None)
    for _ in steps:
        pass
    for g in range(groups):
        down_ref[64 * g : 64 * g + 64, :] += sums[g]
    basis_copy.wait()

    def expand(step, _):
        for k in range(8):
            leaf = step * 8 + k
            mine = down_ref[pl.ds(pl.multiple_of(leaf * 8, 8), 8), :].astype(bf16)
            cols = pl.ds(pl.multiple_of(leaf * 256, 256), 256)
            out_ref[:, cols] = jnp.dot(mine, basis_ref[leaf], preferred_element_type=f32)
        return 0

    lax.fori_loop(0, leaves // 8, expand, 0, unroll=4)


def far_field(devices, place, ids, window, couple, upper, local, basis):
    leaves, rank, leaf_size = basis.shape
    top_levels = devices.bit_length() - 1
    rows = 2 * devices + 16 + -(-3 * top_levels // 16) * 16
    vmem = pl.BlockSpec(memory_space=pltpu.VMEM)
    return pl.pallas_call(
        lambda *refs: far_kernel(devices, *refs),
        grid=(1,),
        out_shape=jax.ShapeDtypeStruct((8, leaves * leaf_size), jnp.float32),
        in_specs=[pl.BlockSpec(memory_space=pltpu.SMEM)]
        + [vmem] * 6
        + [pl.BlockSpec((16, rank * rank), lambda g: (2 * leaves // 16 - 1, 0))]
        + [pl.BlockSpec(memory_space=pltpu.HBM)] * 4,
        out_specs=vmem,
        scratch_shapes=[
            pltpu.VMEM((8 * rank, 384), jnp.bfloat16),
            pltpu.VMEM((rows, 4096), jnp.bfloat16),
            pltpu.VMEM((8 * leaves, rank), jnp.float32),
            pltpu.VMEM(couple.shape, couple.dtype),
            pltpu.VMEM(upper.shape, upper.dtype),
            pltpu.VMEM(basis.shape, basis.dtype),
            pltpu.VMEM((2 * leaves - 16, rank * rank), jnp.bfloat16),
            pltpu.SemaphoreType.DMA((3 + leaves // 8,)),
        ],
        compiler_params=pltpu.CompilerParams(
            vmem_limit_bytes=VMEM_BYTES, dimension_semantics=("arbitrary",)
        ),
        cost_estimate=pl.CostEstimate(flops=2 * 2**28, bytes_accessed=16 * 2**20, transcendentals=0),
        name="far_field",
    )(place, ids, *window, local, local, couple, upper, basis)


def shards(
    points,
    vectors,
    near_list,
    near_count,
    couple_list,
    leaf_basis,
    local_transfer,
    couple_block,
    upper_transfer,
    upper_couple,
):
    devices = lax.axis_size(AXES)
    my_index = lax.axis_index(AXES).astype(jnp.int32)
    leaves, rank, leaf_size = leaf_basis.shape
    couple_slots = couple_list.shape[1]

    local_near = near_list - (my_index - 1) * leaves
    slot = jnp.arange(near_list.shape[1], dtype=jnp.int32)[None, :]
    lists = jnp.where(slot < near_count[:, None], local_near + 1, 0).reshape(-1)
    own = pack_rows(points, vectors, lists)
    place = my_index.reshape(1)
    left = from_behind(own, 1)
    right = from_behind(own, -1)
    local = local_transfer[0]
    coef, upper = up_tree(devices, own, upper_transfer, upper_couple.transpose(1, 0, 2), leaf_basis, local)
    window = [from_behind(coef, d) if d else coef for d in range(REACH, -REACH - 1, -1)]
    upper, left, right = lax.optimization_barrier((upper, left, right))
    upper = lax.all_to_all(upper, AXES, 0, 0, tiled=True)

    near = near_field(devices, place, leaves, near_list.shape[1], left, own, right)
    for_left, near, for_right, upper, window = lax.optimization_barrier((*near, upper, window))
    from_right = from_behind(for_left, -1)
    from_left = from_behind(for_right, 1)

    ids = (couple_list - (my_index - REACH) * leaves).reshape(leaves // 8, 8 * couple_slots)
    couple = couple_block.reshape(leaves * couple_slots, rank * rank)
    far = far_field(
        devices, place, ids, window, couple, upper.reshape(devices * 8, -1), local, leaf_basis
    )
    return far + near + (from_left + from_right)


def solution(mesh):
    placed = (
        P(None, AXES),
        P(None, AXES),
        P(AXES, None),
        P(AXES),
        P(AXES, None),
        P(AXES, None, None),
        P(AXES, None, None),
        P(AXES, None, None),
        P(AXES, None),
        P(AXES, None, None),
    )
    return jax.shard_map(shards, mesh=mesh, in_specs=placed, out_specs=P(None, AXES), check_vma=False)
```

```python
import math

import jax
import jax.numpy as jnp
import numpy as np
from jax import lax
from jax.experimental import pallas as pl
from jax.experimental.pallas import tpu as pltpu
from jax.sharding import PartitionSpec as P

REACH = 2
AXES = ("sect", "dev")
UNROLL = 12
VMEM_BYTES = 58 * 1024 * 1024

soft_sq = 0.0025
even_offsets = (-2, 2, 3)
odd_offsets = (-3, -2, 2)


def from_behind(block, distance):
    devices = range(lax.axis_size(AXES))
    route = [(i - distance, i) for i in devices if i - distance in devices]
    return lax.ppermute(block, AXES, route)


def feature_maps():
    source = np.zeros((32, 16), np.float32)
    target = np.zeros((32, 16), np.float32)
    coords = np.zeros((8, 16), np.float32)
    for c in range(3):
        hi, mid = 8 + c, 11 + c
        source[c, hi] = source[3 + c, hi] = 1.0
        source[6 + c, mid] = source[9 + c, mid] = 1.0
        target[c, hi] = target[6 + c, hi] = -2.0
        target[3 + c, mid] = target[9 + c, mid] = -2.0
        coords[c, hi] = coords[c, mid] = 1.0
    source[15:18, 14] = 1.0
    target[12:15, 14] = 1.0
    return source, coords, target


def split3(x):
    a = x.astype(jnp.bfloat16).astype(jnp.float32)
    b = (x - a).astype(jnp.bfloat16).astype(jnp.float32)
    c = (x - a - b).astype(jnp.bfloat16).astype(jnp.float32)
    return a, b, c


def flow(a, b, only):
    gap = a - b
    return jnp.where((a > 0) & (b > 0) & (gap > 24), (gap * jnp.where(only, 128, 85)) >> 8, 0)


def near_kernel(
    devices,
    place_ref,
    low_bit,
    maps_ref,
    weights_ref,
    left_ref,
    own_ref,
    right_ref,
    left_out,
    own_out,
    right_out,
    s_own,
    s_side,
    t_ref,
    v_own,
    v_side,
    g_even,
    g_odd,
    sum_ref,
    masks_v,
    ids_v,
    masks,
    ids,
    sems,
):
    leaves = own_ref.shape[1] // 256
    slots = weights_ref.shape[0] // leaves
    kernel_scale = 1.0 / math.sqrt(256 * (slots + 1))
    row = lax.broadcasted_iota(jnp.int32, (8, 2048), 0)
    zero = jnp.int32(0)
    f32 = jnp.float32

    def listed(ref):
        return ref[8:16, 0 : leaves * slots].astype(f32)[7:8]

    def band(x, k):
        return jnp.where((x > leaves * k) & (x <= leaves * (k + 1)), 1.0, 0.0)

    mine, theirs_l, theirs_r = listed(own_ref), listed(left_ref), listed(right_ref)
    flags = [band(mine, 1), band(mine, 0), band(mine, 2), band(theirs_l, 2), band(theirs_r, 0)]
    flags += [jnp.where(x > 0.0, 1.0, 0.0) for x in (mine, theirs_l, theirs_r)]
    flags = jnp.concatenate(flags, axis=0).astype(jnp.bfloat16)
    masks_v[...] = jnp.dot(flags, weights_ref[...], preferred_element_type=f32).astype(jnp.int32)
    places = [mine - (leaves + 1.0), theirs_l - (2 * leaves + 1.0), theirs_r - 1.0]
    places += [jnp.zeros((5, leaves * slots), f32)]
    ids_v[...] = jnp.concatenate(places, axis=0).astype(jnp.int32)
    masks_copy = pltpu.make_async_copy(masks_v, masks, sems.at[0])
    ids_copy = pltpu.make_async_copy(ids_v, ids, sems.at[1])
    masks_copy.start()
    ids_copy.start()

    def put_source(ref, chunk, s_ref, v_ref, leaf, target):
        block = ref[:, pl.ds(pl.multiple_of(chunk * 2048, 2048), 2048)]
        wide = jnp.dot(maps_ref[...], block, preferred_element_type=f32)
        coord = wide[32:40]
        norm = jnp.sum(coord * coord, axis=0, keepdims=True)
        a, b, c = split3(norm)
        mixed = jnp.where(row == 7, 1.0, wide[8:16])
        mixed = jnp.where(row == 4, a, jnp.where(row == 5, b, jnp.where(row == 6, c, mixed)))
        rows = jnp.concatenate([wide[0:8], mixed, wide[16:32]], axis=0).astype(jnp.bfloat16)
        for half in range(2):
            quad = [rows[:, 256 * k : 256 * k + 256] for k in range(4 * half, 4 * half + 4)]
            turned = jnp.concatenate(quad, axis=0).T
            for k in range(4):
                s_ref[leaf + 4 * half + k] = turned[:, 32 * k : 32 * k + 32]
        for k in range(8):
            v_ref[leaf + k] = block[:, 256 * k : 256 * k + 256]
        a, b, c = split3(norm + soft_sq)
        first = jnp.where(row == 7, a, wide[48:56])
        second = jnp.where(row == 0, b, jnp.where(row == 1, c, wide[56:64]))
        rows = jnp.concatenate([wide[40:48], first, second, wide[64:72]], axis=0).astype(jnp.bfloat16)
        for k in range(8):
            t_ref[target + k] = rows[:, 256 * k : 256 * k + 256]

    def build_own(chunk, _):
        put_source(own_ref, chunk, s_own, v_own, chunk * 8, chunk * 8)
        return 0

    lax.fori_loop(0, leaves // 8, build_own, 0, unroll=4)
    v_own[leaves] = jnp.zeros((16, 256), jnp.bfloat16)
    v_side[2 * leaves] = jnp.zeros((16, 256), jnp.bfloat16)
    sum_ref[...] = jnp.zeros_like(sum_ref)
    masks_copy.wait()
    ids_copy.wait()

    def pairs(k):
        found = masks[k, 2 * leaves]
        return jnp.where(found > 0, found + leaves, 0)

    here, at_left, at_right = pairs(5), pairs(6), pairs(7)
    me = place_ref[0]

    def whole_rows(k, allowed):
        def fits(carry):
            t, total = carry
            return (t < leaves) & (total + masks[k, leaves + jnp.minimum(t, leaves - 1)] <= allowed)

        def step(carry):
            t, total = carry
            return t + 1, total + masks[k, leaves + t]

        rows, _ = lax.while_loop(fits, step, (jnp.where(allowed > 0, 0, leaves).astype(jnp.int32), zero))
        return jnp.where(allowed > 0, rows, 0)

    give_left = whole_rows(1, flow(here, at_left, at_right == 0))
    give_right = whole_rows(2, flow(here, at_right, at_left == 0))
    take_left = whole_rows(3, flow(at_left, here, me == 1))
    take_right = whole_rows(4, flow(at_right, here, me == devices - 2))

    def mask_of(at, own):
        if own:
            at = jnp.minimum(at, 3 * leaves - 1)
            k = jnp.where(at < leaves, 0, jnp.where(at < 2 * leaves, 3, 4))
            return masks[k, at & (leaves - 1)] | jnp.where(at < leaves, 1 << slots, 0)
        at = jnp.minimum(at, leaves - 1)
        return jnp.where(at < give_left, 0, masks[1, at]) | jnp.where(at < give_right, 0, masks[2, at])

    def after_row(at, own):
        if own:
            return jnp.where(at + 1 == leaves + take_left, 2 * leaves, at + 1)
        return at + 1

    def add_held(held, g_in, v_ref):
        return [jnp.dot(v_ref[held[u][0]], g_in[u], preferred_element_type=f32) for u in range(UNROLL)]

    def put_held(held, updates):
        for u in range(UNROLL):
            sum_ref[held[u][1]] += updates[u][0:8]

    def half(state, held, g_in, g_out, own, end):
        at, mask = state
        fresh = []
        s_ref, v_ref = (s_own, v_own) if own else (s_side, v_side)
        idle = leaves if own else 2 * leaves
        updates = add_held(held, g_in, v_ref)
        for u in range(UNROLL):
            active = at < end
            target = jnp.where(active, at, 0)
            low = mask & -mask
            slot = low_bit[lax.shift_right_logical(low * 0x077CB531, 27)]
            place = ids[target >> (leaves.bit_length() - 1), (target & (leaves - 1)) * slots + jnp.minimum(slot, slots - 1)]
            if own:
                source = jnp.where(slot == slots, target, place)
            else:
                source = jnp.where(place < 0, place + leaves, place)
            used = active & (low != 0)
            source = jnp.where(used, source, 0)
            fresh.append((jnp.where(used, source, idle), target))
            dist = jnp.dot(s_ref[source], t_ref[target], preferred_element_type=f32)
            g_out[u] = lax.rsqrt(dist.astype(jnp.bfloat16))
            rest = mask ^ low
            done = active & (rest == 0)
            following = after_row(at, own)
            mask = jnp.where(done, mask_of(following, own), jnp.where(active, rest, mask))
            at = jnp.where(done, following, at)
        put_held(held, updates)
        return (at, mask), tuple(fresh)

    def both(state, held, own, end):
        state, held = half(state, held, g_even, g_odd, own, end)
        return half(state, held, g_odd, g_even, own, end)

    def nothing(own):
        idle = leaves if own else 2 * leaves
        return tuple((jnp.int32(idle), zero) for _ in range(UNROLL))

    def first_bodies(chunk, carry):
        carry = both(*carry, True, leaves)
        put_source(left_ref, chunk, s_side, v_side, chunk * 8, leaves + chunk * 8)
        put_source(right_ref, chunk, s_side, v_side, leaves + chunk * 8, 2 * leaves + chunk * 8)
        return carry

    def run(own, end, state, held):
        def more(carry):
            return carry[0][0] < end

        state, held = lax.while_loop(more, lambda carry: both(*carry, own, end), (state, held))
        put_held(held, add_held(held, g_even, v_own if own else v_side))

    g_even[...] = jnp.zeros_like(g_even)
    state, held = lax.fori_loop(0, leaves // 8, first_bodies, ((zero, mask_of(zero, True)), nothing(True)))
    run(True, 2 * leaves + take_right, state, held)
    run(False, leaves, (zero, mask_of(zero, False)), nothing(False))

    def finish(chunk, _):
        for k in range(8):
            leaf = chunk * 8 + k
            cols = pl.ds(pl.multiple_of(leaf * 256, 256), 256)
            for side, ref in enumerate((own_out, left_out, right_out)):
                ref[:, cols] = sum_ref[side * leaves + leaf] * kernel_scale
        return 0

    lax.fori_loop(0, leaves // 8, finish, 0)


def near_field(devices, place, leaves, slots, left, own, right):
    points = own.shape[1]
    maps = jnp.asarray(np.concatenate(feature_maps(), axis=0), jnp.bfloat16)
    table = np.zeros((32,), np.int32)
    for bit in range(32):
        table[((0x077CB531 << bit) & 0xFFFFFFFF) >> 27] = bit
    weights = np.zeros((leaves * slots, 256), np.float32)
    for t in range(leaves):
        for k in range(slots):
            weights[t * slots + k, t] = 2.0**k
            weights[t * slots + k, leaves + t] = 1.0
    weights[:, 2 * leaves] = 1.0
    smem = pl.BlockSpec(memory_space=pltpu.SMEM)
    vmem = pl.BlockSpec(memory_space=pltpu.VMEM)
    return pl.pallas_call(
        lambda *refs: near_kernel(devices, *refs),
        out_shape=(jax.ShapeDtypeStruct((8, points), jnp.float32),) * 3,
        in_specs=[smem] * 2 + [vmem] * 5,
        out_specs=(vmem,) * 3,
        scratch_shapes=[
            pltpu.VMEM((leaves, 256, 32), jnp.bfloat16),
            pltpu.VMEM((2 * leaves, 256, 32), jnp.bfloat16),
            pltpu.VMEM((3 * leaves, 32, 256), jnp.bfloat16),
            pltpu.VMEM((leaves + 1, 16, 256), jnp.bfloat16),
            pltpu.VMEM((2 * leaves + 1, 16, 256), jnp.bfloat16),
            pltpu.VMEM((UNROLL, 256, 256), jnp.bfloat16),
            pltpu.VMEM((UNROLL, 256, 256), jnp.bfloat16),
            pltpu.VMEM((3 * leaves, 8, 256), jnp.float32),
            pltpu.VMEM((8, 256), jnp.int32),
            pltpu.VMEM((8, leaves * slots), jnp.int32),
            pltpu.SMEM((8, 256), jnp.int32),
            pltpu.SMEM((8, leaves * slots), jnp.int32),
            pltpu.SemaphoreType.DMA((2,)),
        ],
        compiler_params=pltpu.CompilerParams(vmem_limit_bytes=VMEM_BYTES),
        cost_estimate=pl.CostEstimate(flops=2**31, bytes_accessed=3 * 2**20, transcendentals=0),
        name="near_field",
    )(place, jnp.asarray(table), maps, jnp.asarray(weights, jnp.bfloat16), left, own, right)


def pack_kernel(points_ref, vectors_ref, lists_ref, out_ref):
    rest = jnp.zeros((1, 2048 - lists_ref.shape[1]), jnp.float32)

    def chunk(i, _):
        cols = pl.ds(pl.multiple_of(i * 2048, 2048), 2048)
        centred = points_ref[:, cols] - 0.5
        hi = centred.astype(jnp.bfloat16).astype(jnp.float32)
        mid = centred - hi
        one = jnp.ones((1, 2048), jnp.float32)
        lists = jnp.where(i == 0, jnp.concatenate([lists_ref[...], rest], axis=1), 0.0)
        rows = [vectors_ref[:, cols].astype(jnp.float32), hi, mid, one, lists]
        out_ref[:, cols] = jnp.concatenate(rows, axis=0).astype(jnp.bfloat16)
        return 0

    lax.fori_loop(0, points_ref.shape[1] // 2048, chunk, 0, unroll=2)


def pack_rows(points, vectors, lists):
    lists = lists.astype(jnp.float32)[None]
    vmem = pl.BlockSpec(memory_space=pltpu.VMEM)
    return pl.pallas_call(
        pack_kernel,
        out_shape=jax.ShapeDtypeStruct((16, points.shape[1]), jnp.bfloat16),
        in_specs=[vmem] * 3,
        out_specs=vmem,
        compiler_params=pltpu.CompilerParams(vmem_limit_bytes=VMEM_BYTES),
        cost_estimate=pl.CostEstimate(flops=2**20, bytes_accessed=2**20, transcendentals=0),
        name="pack_rows",
    )(points, vectors, lists)


def spread_map():
    r = lax.broadcasted_iota(jnp.int32, (64, 1024), 0)
    c = lax.broadcasted_iota(jnp.int32, (64, 1024), 1)
    wanted = ((c & 511) >> 4) * 2 + (c >> 9)
    return (r == wanted).astype(jnp.float32).astype(jnp.bfloat16)


def gather_map():
    c = lax.broadcasted_iota(jnp.int32, (1024, 64), 0)
    r = lax.broadcasted_iota(jnp.int32, (1024, 64), 1)
    wanted = ((c & 511) >> 4) * 2 + (c >> 9)
    return (r == wanted).astype(jnp.float32).astype(jnp.bfloat16)


def slot_mask(rows):
    r = lax.broadcasted_iota(jnp.int32, (rows, 1024), 0)
    c = lax.broadcasted_iota(jnp.int32, (rows, 1024), 1)
    return (r >> 3) == (c & 15)


def stacked(rows):
    return jnp.concatenate([rows[:, 128 * j : 128 * j + 128] for j in range(32)], axis=0)


def times_each(coef, blocks, spread, mask):
    wide = jnp.dot(coef, spread, preferred_element_type=jnp.float32)
    wide = jnp.where(mask, wide, 0.0).astype(jnp.bfloat16)
    first = jnp.dot(wide[:, :512], blocks, preferred_element_type=jnp.float32)
    second = jnp.dot(wide[:, 512:], blocks, preferred_element_type=jnp.float32)
    return first[:, :64] + second[:, 64:]


def pair_sum(product):
    rows = product.shape[0]
    pairs = product.reshape(rows // 16, 2, 8, product.shape[1])
    return (pairs[:, 0] + pairs[:, 1]).reshape(rows // 2, product.shape[1])


def doubled(parent):
    rows = parent.shape[0]
    tiles = parent.reshape(rows // 8, 1, 8, parent.shape[1])
    return jnp.concatenate([tiles, tiles], axis=1).reshape(rows * 2, parent.shape[1])


def back_wide(parent, blocks, mask):
    rows = parent.shape[0]
    none = jnp.zeros_like(parent)
    both = jnp.concatenate(
        [jnp.concatenate([parent, none], axis=1), jnp.concatenate([none, parent], axis=1)], axis=0
    ).astype(jnp.bfloat16)
    wide = lax.dot_general(both, blocks, (((1,), (1,)), ((), ())), preferred_element_type=jnp.float32)
    wide = jnp.concatenate([wide[:rows], wide[rows:]], axis=1)
    return jnp.where(mask, wide, 0.0).astype(jnp.bfloat16)


def back_each(parent, blocks, gather, mask):
    return jnp.dot(back_wide(parent, blocks, mask), gather, preferred_element_type=jnp.float32)


def last_rows(local_ref):
    rows = local_ref[local_ref.shape[0] - 16 :, :]
    keep = lax.broadcasted_iota(jnp.int32, rows.shape, 0) < 14
    return jnp.where(keep, rows.astype(jnp.float32), 0.0).astype(jnp.bfloat16)


def up_kernel(
    pack_ref,
    transfer_ref,
    couple_ref,
    last_ref,
    basis_hbm,
    local_hbm,
    coef_ref,
    top_ref,
    flat_ref,
    turn_ref,
    basis_ref,
    local_ref,
    sems,
):
    leaves = basis_ref.shape[0]

    def basis_copy(step):
        part = pl.ds(step * 8, 8)
        return pltpu.make_async_copy(basis_hbm.at[part], basis_ref.at[part], sems.at[step])

    local_copy = pltpu.make_async_copy(
        local_hbm.at[pl.ds(0, 2 * leaves - 16)], local_ref, sems.at[leaves // 8]
    )
    for step in range(leaves // 8):
        basis_copy(step).start()
    local_copy.start()
    spread, mask = spread_map(), slot_mask(128)

    def project(step, _):
        basis_copy(step).wait()
        for k in range(8):
            leaf = step * 8 + k
            block = pack_ref[:, pl.ds(pl.multiple_of(leaf * 256, 256), 256)]
            coef = lax.dot_general(
                block, basis_ref[leaf], (((1,), (1,)), ((), ())), preferred_element_type=jnp.float32
            )
            flat_ref[pl.ds(pl.multiple_of(leaf * 8, 8), 8), :] = coef[0:8]
        return 0

    lax.fori_loop(0, leaves // 8, project, 0, unroll=4)
    local_copy.wait()
    for v in range(8):
        turn_ref[pl.ds(v, 64, stride=8), :] = flat_ref[pl.ds(v, leaves, stride=8), :].T
    coef_ref[...] = turn_ref[...].astype(jnp.bfloat16)
    level = flat_ref[...].astype(jnp.bfloat16)
    width = leaves
    while width > 1:
        start = 2 * leaves - 2 * width
        if width >= 16:
            parts = []
            for g in range(width // 16):
                blocks = stacked(local_ref[start + 16 * g : start + 16 * g + 16, :])
                parts.append(pair_sum(times_each(level[128 * g : 128 * g + 128], blocks, spread, mask)))
            level = jnp.concatenate(parts, axis=0) if len(parts) > 1 else parts[0]
        else:
            first = start - (2 * leaves - 16)
            blocks = stacked(last_rows(last_ref))
            pieces = [level.astype(jnp.float32)]
            if first:
                pieces.insert(0, jnp.zeros((8 * first, 64), jnp.float32))
            rest = 16 - first - width
            if rest:
                pieces.append(jnp.zeros((8 * rest, 64), jnp.float32))
            padded = jnp.concatenate(pieces, axis=0).astype(jnp.bfloat16)
            product = times_each(padded, blocks, spread, mask)
            level = pair_sum(product[8 * first : 8 * (first + width)])
        level = level.astype(jnp.bfloat16)
        width //= 2
    mine = [transfer_ref[...]] + [couple_ref[s] for s in range(3)]
    mine = jnp.concatenate([x.astype(jnp.float32) for x in mine], axis=0).astype(jnp.bfloat16)
    level = jnp.concatenate([level, jnp.zeros_like(level)], axis=1)
    for device in range(top_ref.shape[0]):
        top_ref[device, :, 0:4096] = mine
        top_ref[device, :, 4096:4224] = level


def up_tree(devices, pack, transfer, couple, basis, local):
    leaves, rank, _ = basis.shape
    vmem = pl.BlockSpec(memory_space=pltpu.VMEM)
    return pl.pallas_call(
        up_kernel,
        out_shape=(
            jax.ShapeDtypeStruct((8 * rank, leaves), jnp.bfloat16),
            jax.ShapeDtypeStruct((devices, 8, rank * rank + 128), jnp.bfloat16),
        ),
        grid=(1,),
        in_specs=[
            vmem,
            vmem,
            vmem,
            pl.BlockSpec((16, rank * rank), lambda g: (2 * leaves // 16 - 1, 0)),
            pl.BlockSpec(memory_space=pltpu.HBM),
            pl.BlockSpec(memory_space=pltpu.HBM),
        ],
        out_specs=(vmem, vmem),
        scratch_shapes=[
            pltpu.VMEM((8 * leaves, rank), jnp.float32),
            pltpu.VMEM((8 * rank, leaves), jnp.float32),
            pltpu.VMEM(basis.shape, basis.dtype),
            pltpu.VMEM((2 * leaves - 16, rank * rank), jnp.bfloat16),
            pltpu.SemaphoreType.DMA((leaves // 8 + 1,)),
        ],
        compiler_params=pltpu.CompilerParams(vmem_limit_bytes=VMEM_BYTES),
        cost_estimate=pl.CostEstimate(flops=2 * 2**27, bytes_accessed=4 * 2**20, transcendentals=0),
        name="up_tree",
    )(pack, transfer, couple, local, basis, local)


def far_kernel(
    devices,
    place_ref,
    ids_ref,
    w0,
    w1,
    w2,
    w3,
    w4,
    last_ref,
    local_hbm,
    couple_hbm,
    upper_hbm,
    basis_hbm,
    out_ref,
    window_ref,
    vrows_ref,
    down_ref,
    couple_ref,
    upper_ref,
    basis_ref,
    local_ref,
    sems,
):
    leaves = basis_ref.shape[0]
    groups = leaves // 8
    f32, bf16 = jnp.float32, jnp.bfloat16
    upper_copy = pltpu.make_async_copy(upper_hbm, upper_ref, sems.at[0])
    basis_copy = pltpu.make_async_copy(basis_hbm, basis_ref, sems.at[1])
    local_copy = pltpu.make_async_copy(local_hbm.at[pl.ds(0, 2 * leaves - 16)], local_ref, sems.at[2])
    couple_copies = [
        pltpu.make_async_copy(
            couple_hbm.at[pl.ds(128 * g, 128)], couple_ref.at[pl.ds(128 * g, 128)], sems.at[3 + g]
        )
        for g in range(groups)
    ]
    couple_copies[0].start()
    upper_copy.start()
    for copy in couple_copies[1:]:
        copy.start()
    local_copy.start()
    basis_copy.start()
    for k, ref in enumerate((w0, w1, w2, w3, w4)):
        window_ref[:, 64 * k : 64 * k + 64] = ref[...]
    window_ref[:, 320:384] = jnp.zeros((512, 64), bf16)
    row = lax.broadcasted_iota(jnp.int32, (128, 128), 0)
    col = lax.broadcasted_iota(jnp.int32, (128, 128), 1)
    same = ((row >> 4) == (col >> 4)).astype(f32).astype(bf16)
    leaf_row = lax.broadcasted_iota(jnp.int32, (384, 128), 0)

    def coupling(g):
        couple_copies[g].wait()
        chosen = (leaf_row == ids_ref[g : g + 1, :]).astype(f32).astype(bf16)
        picked = jnp.dot(window_ref[...], chosen, preferred_element_type=f32).astype(bf16)
        summed = jnp.zeros((128, 128), f32)
        for j in range(0, 32, 2):
            left = jnp.concatenate(
                [jnp.concatenate([picked[16 * i : 16 * i + 16]] * 8, axis=0) * same for i in (j, j + 1)], axis=1
            )
            right = jnp.concatenate(
                [couple_ref[128 * g : 128 * g + 128, 128 * i : 128 * i + 128] for i in (j, j + 1)], axis=0
            )
            summed += jnp.dot(left, right, preferred_element_type=f32)
        parts = summed.reshape(8, 2, 8, 128)
        return parts[:, 0, :, :64].reshape(64, 64) + parts[:, 1, :, 64:].reshape(64, 64)

    def tree():
        me = place_ref[0]
        top_levels = devices.bit_length() - 1
        spread, gather, mask = spread_map(), gather_map(), slot_mask(128)
        heap = 2 * devices
        path_slots = 16
        couple_slots = -(-3 * top_levels // 16) * 16
        total = heap + path_slots + couple_slots
        q = lax.broadcasted_iota(jnp.int32, (total, 4 * heap), 0)
        c = lax.broadcasted_iota(jnp.int32, (total, 4 * heap), 1)
        k_v = q - heap
        node_v = jnp.where(q < heap, q, (devices + me) >> jnp.clip(k_v, 0, 31))
        want_v = 8 * (node_v >> 1) + (node_v & 1)
        q_c = q - heap - path_slots
        k_c = (q_c * 11) >> 5
        node_c = (devices + me) >> jnp.clip(k_c, 0, 31)
        want_c = 8 * (node_c >> 1) + 2 + 2 * (q_c - 3 * k_c) + (node_c & 1)
        wanted = jnp.where(q < heap + path_slots, want_v, want_c)
        chosen_rows = (c == wanted).astype(f32).astype(bf16)
        upper_copy.wait()
        for piece in range(8):
            cols = slice(512 * piece, 512 * piece + 512)
            vrows_ref[:, cols] = jnp.dot(chosen_rows, upper_ref[:, cols], preferred_element_type=f32).astype(bf16)
        yield
        top = [None] * top_levels
        level = upper_ref[:, 4096:4160]
        width = devices
        top[0] = level
        for k in range(1, top_levels):
            if width >= 16:
                parts = []
                for g in range(width // 16):
                    blocks = stacked(vrows_ref[width + 16 * g : width + 16 * g + 16, :])
                    parts.append(pair_sum(times_each(level[128 * g : 128 * g + 128], blocks, spread, mask)))
                level = jnp.concatenate(parts, axis=0) if len(parts) > 1 else parts[0]
            else:
                blocks = stacked(vrows_ref[0:16, :])
                pieces = [jnp.zeros((8 * width, 64), f32), level.astype(f32)]
                if 16 - 2 * width:
                    pieces.append(jnp.zeros((8 * (16 - 2 * width), 64), f32))
                padded = jnp.concatenate(pieces, axis=0).astype(bf16)
                product = times_each(padded, blocks, spread, mask)
                level = pair_sum(product[8 * width : 16 * width])
            level = level.astype(bf16)
            top[k] = level
            width //= 2
            yield
        whole = jnp.concatenate(
            [jnp.zeros((16, 64), f32)] + [top[k].astype(f32) for k in range(top_levels - 1, -1, -1)], axis=0
        ).astype(bf16)
        terms = []
        for t in range(couple_slots // 16):
            r = lax.broadcasted_iota(jnp.int32, (128, 8 * heap), 0)
            c = lax.broadcasted_iota(jnp.int32, (128, 8 * heap), 1)
            q = (r >> 3) + 16 * t
            k = (q * 11) >> 5
            s = q - 3 * k
            k = jnp.minimum(k, 31)
            node = me >> k
            odd = (node & 1) == 1
            offset = jnp.where(
                odd,
                jnp.where(s == 0, odd_offsets[0], jnp.where(s == 1, odd_offsets[1], odd_offsets[2])),
                jnp.where(s == 0, even_offsets[0], jnp.where(s == 1, even_offsets[1], even_offsets[2])),
            )
            partner = node + offset
            count = devices >> k
            live = (partner >= 0) & (partner < count) & (k < top_levels)
            want = jnp.where(live, (count + partner) * 8 + (r & 7), -1)
            sources = jnp.dot((c == want).astype(f32).astype(bf16), whole, preferred_element_type=f32).astype(bf16)
            blocks = stacked(vrows_ref[heap + path_slots + 16 * t : heap + path_slots + 16 * t + 16, :])
            product = times_each(sources, blocks, spread, mask)
            terms.extend(product[8 * i : 8 * i + 8] for i in range(16))
        yield
        path_blocks = stacked(vrows_ref[heap : heap + path_slots, :])
        lane = lax.broadcasted_iota(jnp.int32, (8, 1024), 1)
        parent = None
        for k in range(top_levels - 1, -1, -1):
            value = terms[3 * k] + terms[3 * k + 1] + terms[3 * k + 2]
            if parent is not None:
                value = value + back_each(parent, path_blocks, gather, (lane & 15) == k)
            parent = value.astype(bf16).astype(f32)
            yield
        local_copy.wait()
        width = 2
        while width <= leaves:
            start = 2 * leaves - 2 * width
            if width >= 16:
                parts = []
                for g in range(width // 16):
                    blocks = stacked(local_ref[start + 16 * g : start + 16 * g + 16, :])
                    pair = doubled(parent[64 * g : 64 * g + 64])
                    parts.append(back_wide(pair, blocks, mask))
                wide = jnp.concatenate(parts, axis=0) if len(parts) > 1 else parts[0]
                parent = jnp.dot(wide, gather, preferred_element_type=f32)
            else:
                first = start - (2 * leaves - 16)
                blocks = stacked(last_rows(last_ref))
                pieces = [doubled(parent)]
                if first:
                    pieces.insert(0, jnp.zeros((8 * first, 64), f32))
                rest = 16 - first - width
                if rest:
                    pieces.append(jnp.zeros((8 * rest, 64), f32))
                parent = back_each(jnp.concatenate(pieces, axis=0), blocks, gather, mask)
                parent = parent[8 * first : 8 * (first + width)]
            width *= 2
            if width <= leaves:
                yield
        down_ref[...] = parent

    steps = tree()
    sums = []
    for g in range(groups):
        sums.append(coupling(g))
        for _ in range(2):
            next(steps, None)
    for _ in steps:
        pass
    for g in range(groups):
        down_ref[64 * g : 64 * g + 64, :] += sums[g]
    basis_copy.wait()

    def expand(step, _):
        for k in range(8):
            leaf = step * 8 + k
            mine = down_ref[pl.ds(pl.multiple_of(leaf * 8, 8), 8), :].astype(bf16)
            cols = pl.ds(pl.multiple_of(leaf * 256, 256), 256)
            out_ref[:, cols] = jnp.dot(mine, basis_ref[leaf], preferred_element_type=f32)
        return 0

    lax.fori_loop(0, leaves // 8, expand, 0, unroll=4)


def far_field(devices, place, ids, window, couple, upper, local, basis):
    leaves, rank, leaf_size = basis.shape
    top_levels = devices.bit_length() - 1
    rows = 2 * devices + 16 + -(-3 * top_levels // 16) * 16
    vmem = pl.BlockSpec(memory_space=pltpu.VMEM)
    return pl.pallas_call(
        lambda *refs: far_kernel(devices, *refs),
        grid=(1,),
        out_shape=jax.ShapeDtypeStruct((8, leaves * leaf_size), jnp.float32),
        in_specs=[pl.BlockSpec(memory_space=pltpu.SMEM)]
        + [vmem] * 6
        + [pl.BlockSpec((16, rank * rank), lambda g: (2 * leaves // 16 - 1, 0))]
        + [pl.BlockSpec(memory_space=pltpu.HBM)] * 4,
        out_specs=vmem,
        scratch_shapes=[
            pltpu.VMEM((8 * rank, 384), jnp.bfloat16),
            pltpu.VMEM((rows, 4096), jnp.bfloat16),
            pltpu.VMEM((8 * leaves, rank), jnp.float32),
            pltpu.VMEM(couple.shape, couple.dtype),
            pltpu.VMEM(upper.shape, upper.dtype),
            pltpu.VMEM(basis.shape, basis.dtype),
            pltpu.VMEM((2 * leaves - 16, rank * rank), jnp.bfloat16),
            pltpu.SemaphoreType.DMA((3 + leaves // 8,)),
        ],
        compiler_params=pltpu.CompilerParams(
            vmem_limit_bytes=VMEM_BYTES, dimension_semantics=("arbitrary",)
        ),
        cost_estimate=pl.CostEstimate(flops=2 * 2**28, bytes_accessed=16 * 2**20, transcendentals=0),
        name="far_field",
    )(place, ids, *window, local, local, couple, upper, basis)


def shards(
    points,
    vectors,
    near_list,
    near_count,
    couple_list,
    leaf_basis,
    local_transfer,
    couple_block,
    upper_transfer,
    upper_couple,
):
    devices = lax.axis_size(AXES)
    my_index = lax.axis_index(AXES).astype(jnp.int32)
    leaves, rank, leaf_size = leaf_basis.shape
    couple_slots = couple_list.shape[1]

    local_near = near_list - (my_index - 1) * leaves
    slot = jnp.arange(near_list.shape[1], dtype=jnp.int32)[None, :]
    lists = jnp.where(slot < near_count[:, None], local_near + 1, 0).reshape(-1)
    own = pack_rows(points, vectors, lists)
    place = my_index.reshape(1)
    left = from_behind(own, 1)
    right = from_behind(own, -1)
    local = local_transfer[0]
    coef, upper = up_tree(devices, own, upper_transfer, upper_couple.transpose(1, 0, 2), leaf_basis, local)
    window = [from_behind(coef, d) if d else coef for d in range(REACH, -REACH - 1, -1)]
    upper, left, right = lax.optimization_barrier((upper, left, right))
    upper = lax.all_to_all(upper, AXES, 0, 0, tiled=True)

    near = near_field(devices, place, leaves, near_list.shape[1], left, own, right)
    for_left, near, for_right, upper, window = lax.optimization_barrier((*near, upper, window))
    from_right = from_behind(for_left, -1)
    from_left = from_behind(for_right, 1)

    ids = (couple_list - (my_index - REACH) * leaves).reshape(leaves // 8, 8 * couple_slots)
    couple = couple_block.reshape(leaves * couple_slots, rank * rank)
    far = far_field(
        devices, place, ids, window, couple, upper.reshape(devices * 8, -1), local, leaf_basis
    )
    return far + near + (from_left + from_right)


def solution(mesh):
    placed = (
        P(None, AXES),
        P(None, AXES),
        P(AXES, None),
        P(AXES),
        P(AXES, None),
        P(AXES, None, None),
        P(AXES, None, None),
        P(AXES, None, None),
        P(AXES, None),
        P(AXES, None, None),
    )
    return jax.shard_map(shards, mesh=mesh, in_specs=placed, out_specs=P(None, AXES), check_vma=False)
```

```python
import math

import jax
import jax.numpy as jnp
import numpy as np
from jax import lax
from jax.experimental import pallas as pl
from jax.experimental.pallas import tpu as pltpu
from jax.sharding import PartitionSpec as P

REACH = 2
AXES = ("sect", "dev")
UNROLL = 16
VMEM_BYTES = 58 * 1024 * 1024

soft_sq = 0.0025
even_offsets = (-2, 2, 3)
odd_offsets = (-3, -2, 2)


def from_behind(block, distance):
    devices = range(lax.axis_size(AXES))
    route = [(i - distance, i) for i in devices if i - distance in devices]
    return lax.ppermute(block, AXES, route)


def feature_maps():
    source = np.zeros((32, 16), np.float32)
    target = np.zeros((32, 16), np.float32)
    coords = np.zeros((8, 16), np.float32)
    for c in range(3):
        hi, mid = 8 + c, 11 + c
        source[c, hi] = source[3 + c, hi] = 1.0
        source[6 + c, mid] = source[9 + c, mid] = 1.0
        target[c, hi] = target[6 + c, hi] = -2.0
        target[3 + c, mid] = target[9 + c, mid] = -2.0
        coords[c, hi] = coords[c, mid] = 1.0
    source[15:18, 14] = 1.0
    target[12:15, 14] = 1.0
    return source, coords, target


def split3(x):
    a = x.astype(jnp.bfloat16).astype(jnp.float32)
    b = (x - a).astype(jnp.bfloat16).astype(jnp.float32)
    c = (x - a - b).astype(jnp.bfloat16).astype(jnp.float32)
    return a, b, c


def flow(a, b, only):
    gap = a - b
    return jnp.where((a > 0) & (b > 0) & (gap > 24), (gap * jnp.where(only, 128, 85)) >> 8, 0)


def near_kernel(
    devices,
    place_ref,
    low_bit,
    maps_ref,
    weights_ref,
    left_ref,
    own_ref,
    right_ref,
    left_out,
    own_out,
    right_out,
    s_own,
    s_side,
    t_ref,
    v_own,
    v_side,
    g_even,
    g_odd,
    sum_ref,
    masks_v,
    ids_v,
    masks,
    ids,
    sems,
):
    leaves = own_ref.shape[1] // 256
    slots = weights_ref.shape[0] // leaves
    kernel_scale = 1.0 / math.sqrt(256 * (slots + 1))
    row = lax.broadcasted_iota(jnp.int32, (8, 2048), 0)
    zero = jnp.int32(0)
    f32 = jnp.float32

    def listed(ref):
        return ref[8:16, 0 : leaves * slots].astype(f32)[7:8]

    def band(x, k):
        return jnp.where((x > leaves * k) & (x <= leaves * (k + 1)), 1.0, 0.0)

    mine, theirs_l, theirs_r = listed(own_ref), listed(left_ref), listed(right_ref)
    flags = [band(mine, 1), band(mine, 0), band(mine, 2), band(theirs_l, 2), band(theirs_r, 0)]
    flags += [jnp.where(x > 0.0, 1.0, 0.0) for x in (mine, theirs_l, theirs_r)]
    flags = jnp.concatenate(flags, axis=0).astype(jnp.bfloat16)
    masks_v[...] = jnp.dot(flags, weights_ref[...], preferred_element_type=f32).astype(jnp.int32)
    places = [mine - (leaves + 1.0), theirs_l - (2 * leaves + 1.0), theirs_r - 1.0]
    places += [jnp.zeros((5, leaves * slots), f32)]
    ids_v[...] = jnp.concatenate(places, axis=0).astype(jnp.int32)
    masks_copy = pltpu.make_async_copy(masks_v, masks, sems.at[0])
    ids_copy = pltpu.make_async_copy(ids_v, ids, sems.at[1])
    masks_copy.start()
    ids_copy.start()

    def put_source(ref, chunk, s_ref, v_ref, leaf, target):
        block = ref[:, pl.ds(pl.multiple_of(chunk * 2048, 2048), 2048)]
        wide = jnp.dot(maps_ref[...], block, preferred_element_type=f32)
        coord = wide[32:40]
        norm = jnp.sum(coord * coord, axis=0, keepdims=True)
        a, b, c = split3(norm)
        mixed = jnp.where(row == 7, 1.0, wide[8:16])
        mixed = jnp.where(row == 4, a, jnp.where(row == 5, b, jnp.where(row == 6, c, mixed)))
        rows = jnp.concatenate([wide[0:8], mixed, wide[16:32]], axis=0).astype(jnp.bfloat16)
        for half in range(2):
            quad = [rows[:, 256 * k : 256 * k + 256] for k in range(4 * half, 4 * half + 4)]
            turned = jnp.concatenate(quad, axis=0).T
            for k in range(4):
                s_ref[leaf + 4 * half + k] = turned[:, 32 * k : 32 * k + 32]
        for k in range(8):
            v_ref[leaf + k] = block[:, 256 * k : 256 * k + 256]
        a, b, c = split3(norm + soft_sq)
        first = jnp.where(row == 7, a, wide[48:56])
        second = jnp.where(row == 0, b, jnp.where(row == 1, c, wide[56:64]))
        rows = jnp.concatenate([wide[40:48], first, second, wide[64:72]], axis=0).astype(jnp.bfloat16)
        for k in range(8):
            t_ref[target + k] = rows[:, 256 * k : 256 * k + 256]

    def build_own(chunk, _):
        put_source(own_ref, chunk, s_own, v_own, chunk * 8, chunk * 8)
        return 0

    lax.fori_loop(0, leaves // 8, build_own, 0, unroll=4)
    v_own[leaves] = jnp.zeros((16, 256), jnp.bfloat16)
    v_side[2 * leaves] = jnp.zeros((16, 256), jnp.bfloat16)
    sum_ref[...] = jnp.zeros_like(sum_ref)
    masks_copy.wait()
    ids_copy.wait()

    def pairs(k):
        found = masks[k, 2 * leaves]
        return jnp.where(found > 0, found + leaves, 0)

    here, at_left, at_right = pairs(5), pairs(6), pairs(7)
    me = place_ref[0]

    def whole_rows(k, allowed):
        def fits(carry):
            t, total = carry
            return (t < leaves) & (total + masks[k, leaves + jnp.minimum(t, leaves - 1)] <= allowed)

        def step(carry):
            t, total = carry
            return t + 1, total + masks[k, leaves + t]

        rows, _ = lax.while_loop(fits, step, (jnp.where(allowed > 0, 0, leaves).astype(jnp.int32), zero))
        return jnp.where(allowed > 0, rows, 0)

    give_left = whole_rows(1, flow(here, at_left, at_right == 0))
    give_right = whole_rows(2, flow(here, at_right, at_left == 0))
    take_left = whole_rows(3, flow(at_left, here, me == 1))
    take_right = whole_rows(4, flow(at_right, here, me == devices - 2))

    def mask_of(at, own):
        if own:
            at = jnp.minimum(at, 3 * leaves - 1)
            k = jnp.where(at < leaves, 0, jnp.where(at < 2 * leaves, 3, 4))
            return masks[k, at & (leaves - 1)] | jnp.where(at < leaves, 1 << slots, 0)
        at = jnp.minimum(at, leaves - 1)
        return jnp.where(at < give_left, 0, masks[1, at]) | jnp.where(at < give_right, 0, masks[2, at])

    def after_row(at, own):
        if own:
            return jnp.where(at + 1 == leaves + take_left, 2 * leaves, at + 1)
        return at + 1

    def add_held(held, g_in, v_ref):
        return [jnp.dot(v_ref[held[u][0]], g_in[u], preferred_element_type=f32) for u in range(UNROLL)]

    def put_held(held, updates):
        for u in range(UNROLL):
            sum_ref[held[u][1]] += updates[u][0:8]

    def half(state, held, g_in, g_out, own, end):
        at, mask = state
        fresh = []
        s_ref, v_ref = (s_own, v_own) if own else (s_side, v_side)
        idle = leaves if own else 2 * leaves
        updates = add_held(held, g_in, v_ref)
        for u in range(UNROLL):
            active = at < end
            target = jnp.where(active, at, 0)
            low = mask & -mask
            slot = low_bit[lax.shift_right_logical(low * 0x077CB531, 27)]
            place = ids[target >> (leaves.bit_length() - 1), (target & (leaves - 1)) * slots + jnp.minimum(slot, slots - 1)]
            if own:
                source = jnp.where(slot == slots, target, place)
            else:
                source = jnp.where(place < 0, place + leaves, place)
            used = active & (low != 0)
            source = jnp.where(used, source, 0)
            fresh.append((jnp.where(used, source, idle), target))
            dist = jnp.dot(s_ref[source], t_ref[target], preferred_element_type=f32)
            g_out[u] = lax.rsqrt(dist.astype(jnp.bfloat16))
            rest = mask ^ low
            done = active & (rest == 0)
            following = after_row(at, own)
            mask = jnp.where(done, mask_of(following, own), jnp.where(active, rest, mask))
            at = jnp.where(done, following, at)
        put_held(held, updates)
        return (at, mask), tuple(fresh)

    def both(state, held, own, end):
        state, held = half(state, held, g_even, g_odd, own, end)
        return half(state, held, g_odd, g_even, own, end)

    def nothing(own):
        idle = leaves if own else 2 * leaves
        return tuple((jnp.int32(idle), zero) for _ in range(UNROLL))

    def first_bodies(chunk, carry):
        carry = both(*carry, True, leaves)
        put_source(left_ref, chunk, s_side, v_side, chunk * 8, leaves + chunk * 8)
        put_source(right_ref, chunk, s_side, v_side, leaves + chunk * 8, 2 * leaves + chunk * 8)
        return carry

    def run(own, end, state, held):
        def more(carry):
            return carry[0][0] < end

        state, held = lax.while_loop(more, lambda carry: both(*carry, own, end), (state, held))
        put_held(held, add_held(held, g_even, v_own if own else v_side))

    g_even[...] = jnp.zeros_like(g_even)
    state, held = lax.fori_loop(0, leaves // 8, first_bodies, ((zero, mask_of(zero, True)), nothing(True)))
    run(True, 2 * leaves + take_right, state, held)
    run(False, leaves, (zero, mask_of(zero, False)), nothing(False))

    def finish(chunk, _):
        for k in range(8):
            leaf = chunk * 8 + k
            cols = pl.ds(pl.multiple_of(leaf * 256, 256), 256)
            for side, ref in enumerate((own_out, left_out, right_out)):
                ref[:, cols] = sum_ref[side * leaves + leaf] * kernel_scale
        return 0

    lax.fori_loop(0, leaves // 8, finish, 0)


def near_field(devices, place, leaves, slots, left, own, right):
    points = own.shape[1]
    maps = jnp.asarray(np.concatenate(feature_maps(), axis=0), jnp.bfloat16)
    table = np.zeros((32,), np.int32)
    for bit in range(32):
        table[((0x077CB531 << bit) & 0xFFFFFFFF) >> 27] = bit
    weights = np.zeros((leaves * slots, 256), np.float32)
    for t in range(leaves):
        for k in range(slots):
            weights[t * slots + k, t] = 2.0**k
            weights[t * slots + k, leaves + t] = 1.0
    weights[:, 2 * leaves] = 1.0
    smem = pl.BlockSpec(memory_space=pltpu.SMEM)
    vmem = pl.BlockSpec(memory_space=pltpu.VMEM)
    return pl.pallas_call(
        lambda *refs: near_kernel(devices, *refs),
        out_shape=(jax.ShapeDtypeStruct((8, points), jnp.float32),) * 3,
        in_specs=[smem] * 2 + [vmem] * 5,
        out_specs=(vmem,) * 3,
        scratch_shapes=[
            pltpu.VMEM((leaves, 256, 32), jnp.bfloat16),
            pltpu.VMEM((2 * leaves, 256, 32), jnp.bfloat16),
            pltpu.VMEM((3 * leaves, 32, 256), jnp.bfloat16),
            pltpu.VMEM((leaves + 1, 16, 256), jnp.bfloat16),
            pltpu.VMEM((2 * leaves + 1, 16, 256), jnp.bfloat16),
            pltpu.VMEM((UNROLL, 256, 256), jnp.bfloat16),
            pltpu.VMEM((UNROLL, 256, 256), jnp.bfloat16),
            pltpu.VMEM((3 * leaves, 8, 256), jnp.float32),
            pltpu.VMEM((8, 256), jnp.int32),
            pltpu.VMEM((8, leaves * slots), jnp.int32),
            pltpu.SMEM((8, 256), jnp.int32),
            pltpu.SMEM((8, leaves * slots), jnp.int32),
            pltpu.SemaphoreType.DMA((2,)),
        ],
        compiler_params=pltpu.CompilerParams(vmem_limit_bytes=VMEM_BYTES),
        cost_estimate=pl.CostEstimate(flops=2**31, bytes_accessed=3 * 2**20, transcendentals=0),
        name="near_field",
    )(place, jnp.asarray(table), maps, jnp.asarray(weights, jnp.bfloat16), left, own, right)


def pack_kernel(points_ref, vectors_ref, lists_ref, out_ref):
    rest = jnp.zeros((1, 2048 - lists_ref.shape[1]), jnp.float32)

    def chunk(i, _):
        cols = pl.ds(pl.multiple_of(i * 2048, 2048), 2048)
        centred = points_ref[:, cols] - 0.5
        hi = centred.astype(jnp.bfloat16).astype(jnp.float32)
        mid = centred - hi
        one = jnp.ones((1, 2048), jnp.float32)
        lists = jnp.where(i == 0, jnp.concatenate([lists_ref[...], rest], axis=1), 0.0)
        rows = [vectors_ref[:, cols].astype(jnp.float32), hi, mid, one, lists]
        out_ref[:, cols] = jnp.concatenate(rows, axis=0).astype(jnp.bfloat16)
        return 0

    lax.fori_loop(0, points_ref.shape[1] // 2048, chunk, 0, unroll=2)


def pack_rows(points, vectors, lists):
    lists = lists.astype(jnp.float32)[None]
    vmem = pl.BlockSpec(memory_space=pltpu.VMEM)
    return pl.pallas_call(
        pack_kernel,
        out_shape=jax.ShapeDtypeStruct((16, points.shape[1]), jnp.bfloat16),
        in_specs=[vmem] * 3,
        out_specs=vmem,
        compiler_params=pltpu.CompilerParams(vmem_limit_bytes=VMEM_BYTES),
        cost_estimate=pl.CostEstimate(flops=2**20, bytes_accessed=2**20, transcendentals=0),
        name="pack_rows",
    )(points, vectors, lists)


def spread_map():
    r = lax.broadcasted_iota(jnp.int32, (64, 1024), 0)
    c = lax.broadcasted_iota(jnp.int32, (64, 1024), 1)
    wanted = ((c & 511) >> 4) * 2 + (c >> 9)
    return (r == wanted).astype(jnp.float32).astype(jnp.bfloat16)


def gather_map():
    c = lax.broadcasted_iota(jnp.int32, (1024, 64), 0)
    r = lax.broadcasted_iota(jnp.int32, (1024, 64), 1)
    wanted = ((c & 511) >> 4) * 2 + (c >> 9)
    return (r == wanted).astype(jnp.float32).astype(jnp.bfloat16)


def slot_mask(rows):
    r = lax.broadcasted_iota(jnp.int32, (rows, 1024), 0)
    c = lax.broadcasted_iota(jnp.int32, (rows, 1024), 1)
    return (r >> 3) == (c & 15)


def stacked(rows):
    return jnp.concatenate([rows[:, 128 * j : 128 * j + 128] for j in range(32)], axis=0)


def times_each(coef, blocks, spread, mask):
    wide = jnp.dot(coef, spread, preferred_element_type=jnp.float32)
    wide = jnp.where(mask, wide, 0.0).astype(jnp.bfloat16)
    first = jnp.dot(wide[:, :512], blocks, preferred_element_type=jnp.float32)
    second = jnp.dot(wide[:, 512:], blocks, preferred_element_type=jnp.float32)
    return first[:, :64] + second[:, 64:]


def pair_sum(product):
    rows = product.shape[0]
    pairs = product.reshape(rows // 16, 2, 8, product.shape[1])
    return (pairs[:, 0] + pairs[:, 1]).reshape(rows // 2, product.shape[1])


def doubled(parent):
    rows = parent.shape[0]
    tiles = parent.reshape(rows // 8, 1, 8, parent.shape[1])
    return jnp.concatenate([tiles, tiles], axis=1).reshape(rows * 2, parent.shape[1])


def back_wide(parent, blocks, mask):
    rows = parent.shape[0]
    none = jnp.zeros_like(parent)
    both = jnp.concatenate(
        [jnp.concatenate([parent, none], axis=1), jnp.concatenate([none, parent], axis=1)], axis=0
    ).astype(jnp.bfloat16)
    wide = lax.dot_general(both, blocks, (((1,), (1,)), ((), ())), preferred_element_type=jnp.float32)
    wide = jnp.concatenate([wide[:rows], wide[rows:]], axis=1)
    return jnp.where(mask, wide, 0.0).astype(jnp.bfloat16)


def back_each(parent, blocks, gather, mask):
    return jnp.dot(back_wide(parent, blocks, mask), gather, preferred_element_type=jnp.float32)


def last_rows(local_ref):
    rows = local_ref[local_ref.shape[0] - 16 :, :]
    keep = lax.broadcasted_iota(jnp.int32, rows.shape, 0) < 14
    return jnp.where(keep, rows.astype(jnp.float32), 0.0).astype(jnp.bfloat16)


def up_kernel(
    pack_ref,
    transfer_ref,
    couple_ref,
    last_ref,
    basis_hbm,
    local_hbm,
    coef_ref,
    top_ref,
    flat_ref,
    turn_ref,
    basis_ref,
    local_ref,
    sems,
):
    leaves = basis_ref.shape[0]

    def basis_copy(step):
        part = pl.ds(step * 8, 8)
        return pltpu.make_async_copy(basis_hbm.at[part], basis_ref.at[part], sems.at[step])

    local_copy = pltpu.make_async_copy(
        local_hbm.at[pl.ds(0, 2 * leaves - 16)], local_ref, sems.at[leaves // 8]
    )
    for step in range(leaves // 8):
        basis_copy(step).start()
    local_copy.start()
    spread, mask = spread_map(), slot_mask(128)

    def project(step, _):
        basis_copy(step).wait()
        for k in range(8):
            leaf = step * 8 + k
            block = pack_ref[:, pl.ds(pl.multiple_of(leaf * 256, 256), 256)]
            coef = lax.dot_general(
                block, basis_ref[leaf], (((1,), (1,)), ((), ())), preferred_element_type=jnp.float32
            )
            flat_ref[pl.ds(pl.multiple_of(leaf * 8, 8), 8), :] = coef[0:8]
        return 0

    lax.fori_loop(0, leaves // 8, project, 0, unroll=4)
    local_copy.wait()
    for v in range(8):
        turn_ref[pl.ds(v, 64, stride=8), :] = flat_ref[pl.ds(v, leaves, stride=8), :].T
    coef_ref[...] = turn_ref[...].astype(jnp.bfloat16)
    level = flat_ref[...].astype(jnp.bfloat16)
    width = leaves
    while width > 1:
        start = 2 * leaves - 2 * width
        if width >= 16:
            parts = []
            for g in range(width // 16):
                blocks = stacked(local_ref[start + 16 * g : start + 16 * g + 16, :])
                parts.append(pair_sum(times_each(level[128 * g : 128 * g + 128], blocks, spread, mask)))
            level = jnp.concatenate(parts, axis=0) if len(parts) > 1 else parts[0]
        else:
            first = start - (2 * leaves - 16)
            blocks = stacked(last_rows(last_ref))
            pieces = [level.astype(jnp.float32)]
            if first:
                pieces.insert(0, jnp.zeros((8 * first, 64), jnp.float32))
            rest = 16 - first - width
            if rest:
                pieces.append(jnp.zeros((8 * rest, 64), jnp.float32))
            padded = jnp.concatenate(pieces, axis=0).astype(jnp.bfloat16)
            product = times_each(padded, blocks, spread, mask)
            level = pair_sum(product[8 * first : 8 * (first + width)])
        level = level.astype(jnp.bfloat16)
        width //= 2
    mine = [transfer_ref[...]] + [couple_ref[s] for s in range(3)]
    mine = jnp.concatenate([x.astype(jnp.float32) for x in mine], axis=0).astype(jnp.bfloat16)
    level = jnp.concatenate([level, jnp.zeros_like(level)], axis=1)
    for device in range(top_ref.shape[0]):
        top_ref[device, :, 0:4096] = mine
        top_ref[device, :, 4096:4224] = level


def up_tree(devices, pack, transfer, couple, basis, local):
    leaves, rank, _ = basis.shape
    vmem = pl.BlockSpec(memory_space=pltpu.VMEM)
    return pl.pallas_call(
        up_kernel,
        out_shape=(
            jax.ShapeDtypeStruct((8 * rank, leaves), jnp.bfloat16),
            jax.ShapeDtypeStruct((devices, 8, rank * rank + 128), jnp.bfloat16),
        ),
        grid=(1,),
        in_specs=[
            vmem,
            vmem,
            vmem,
            pl.BlockSpec((16, rank * rank), lambda g: (2 * leaves // 16 - 1, 0)),
            pl.BlockSpec(memory_space=pltpu.HBM),
            pl.BlockSpec(memory_space=pltpu.HBM),
        ],
        out_specs=(vmem, vmem),
        scratch_shapes=[
            pltpu.VMEM((8 * leaves, rank), jnp.float32),
            pltpu.VMEM((8 * rank, leaves), jnp.float32),
            pltpu.VMEM(basis.shape, basis.dtype),
            pltpu.VMEM((2 * leaves - 16, rank * rank), jnp.bfloat16),
            pltpu.SemaphoreType.DMA((leaves // 8 + 1,)),
        ],
        compiler_params=pltpu.CompilerParams(vmem_limit_bytes=VMEM_BYTES),
        cost_estimate=pl.CostEstimate(flops=2 * 2**27, bytes_accessed=4 * 2**20, transcendentals=0),
        name="up_tree",
    )(pack, transfer, couple, local, basis, local)


def far_kernel(
    devices,
    place_ref,
    ids_ref,
    w0,
    w1,
    w2,
    w3,
    w4,
    last_ref,
    local_hbm,
    couple_hbm,
    upper_hbm,
    basis_hbm,
    out_ref,
    window_ref,
    vrows_ref,
    down_ref,
    couple_ref,
    upper_ref,
    basis_ref,
    local_ref,
    sems,
):
    leaves = basis_ref.shape[0]
    groups = leaves // 8
    f32, bf16 = jnp.float32, jnp.bfloat16
    upper_copy = pltpu.make_async_copy(upper_hbm, upper_ref, sems.at[0])
    basis_copy = pltpu.make_async_copy(basis_hbm, basis_ref, sems.at[1])
    local_copy = pltpu.make_async_copy(local_hbm.at[pl.ds(0, 2 * leaves - 16)], local_ref, sems.at[2])
    couple_copies = [
        pltpu.make_async_copy(
            couple_hbm.at[pl.ds(128 * g, 128)], couple_ref.at[pl.ds(128 * g, 128)], sems.at[3 + g]
        )
        for g in range(groups)
    ]
    couple_copies[0].start()
    upper_copy.start()
    for copy in couple_copies[1:]:
        copy.start()
    local_copy.start()
    basis_copy.start()
    for k, ref in enumerate((w0, w1, w2, w3, w4)):
        window_ref[:, 64 * k : 64 * k + 64] = ref[...]
    window_ref[:, 320:384] = jnp.zeros((512, 64), bf16)
    row = lax.broadcasted_iota(jnp.int32, (128, 128), 0)
    col = lax.broadcasted_iota(jnp.int32, (128, 128), 1)
    same = ((row >> 4) == (col >> 4)).astype(f32).astype(bf16)
    leaf_row = lax.broadcasted_iota(jnp.int32, (384, 128), 0)

    def coupling(g):
        couple_copies[g].wait()
        chosen = (leaf_row == ids_ref[g : g + 1, :]).astype(f32).astype(bf16)
        picked = jnp.dot(window_ref[...], chosen, preferred_element_type=f32).astype(bf16)
        summed = jnp.zeros((128, 128), f32)
        for j in range(0, 32, 2):
            left = jnp.concatenate(
                [jnp.concatenate([picked[16 * i : 16 * i + 16]] * 8, axis=0) * same for i in (j, j + 1)], axis=1
            )
            right = jnp.concatenate(
                [couple_ref[128 * g : 128 * g + 128, 128 * i : 128 * i + 128] for i in (j, j + 1)], axis=0
            )
            summed += jnp.dot(left, right, preferred_element_type=f32)
        parts = summed.reshape(8, 2, 8, 128)
        return parts[:, 0, :, :64].reshape(64, 64) + parts[:, 1, :, 64:].reshape(64, 64)

    def tree():
        me = place_ref[0]
        top_levels = devices.bit_length() - 1
        spread, gather, mask = spread_map(), gather_map(), slot_mask(128)
        heap = 2 * devices
        path_slots = 16
        couple_slots = -(-3 * top_levels // 16) * 16
        total = heap + path_slots + couple_slots
        q = lax.broadcasted_iota(jnp.int32, (total, 4 * heap), 0)
        c = lax.broadcasted_iota(jnp.int32, (total, 4 * heap), 1)
        k_v = q - heap
        node_v = jnp.where(q < heap, q, (devices + me) >> jnp.clip(k_v, 0, 31))
        want_v = 8 * (node_v >> 1) + (node_v & 1)
        q_c = q - heap - path_slots
        k_c = (q_c * 11) >> 5
        node_c = (devices + me) >> jnp.clip(k_c, 0, 31)
        want_c = 8 * (node_c >> 1) + 2 + 2 * (q_c - 3 * k_c) + (node_c & 1)
        wanted = jnp.where(q < heap + path_slots, want_v, want_c)
        chosen_rows = (c == wanted).astype(f32).astype(bf16)
        upper_copy.wait()
        for piece in range(8):
            cols = slice(512 * piece, 512 * piece + 512)
            vrows_ref[:, cols] = jnp.dot(chosen_rows, upper_ref[:, cols], preferred_element_type=f32).astype(bf16)
        yield
        top = [None] * top_levels
        level = upper_ref[:, 4096:4160]
        width = devices
        top[0] = level
        for k in range(1, top_levels):
            if width >= 16:
                parts = []
                for g in range(width // 16):
                    blocks = stacked(vrows_ref[width + 16 * g : width + 16 * g + 16, :])
                    parts.append(pair_sum(times_each(level[128 * g : 128 * g + 128], blocks, spread, mask)))
                level = jnp.concatenate(parts, axis=0) if len(parts) > 1 else parts[0]
            else:
                blocks = stacked(vrows_ref[0:16, :])
                pieces = [jnp.zeros((8 * width, 64), f32), level.astype(f32)]
                if 16 - 2 * width:
                    pieces.append(jnp.zeros((8 * (16 - 2 * width), 64), f32))
                padded = jnp.concatenate(pieces, axis=0).astype(bf16)
                product = times_each(padded, blocks, spread, mask)
                level = pair_sum(product[8 * width : 16 * width])
            level = level.astype(bf16)
            top[k] = level
            width //= 2
            yield
        whole = jnp.concatenate(
            [jnp.zeros((16, 64), f32)] + [top[k].astype(f32) for k in range(top_levels - 1, -1, -1)], axis=0
        ).astype(bf16)
        terms = []
        for t in range(couple_slots // 16):
            r = lax.broadcasted_iota(jnp.int32, (128, 8 * heap), 0)
            c = lax.broadcasted_iota(jnp.int32, (128, 8 * heap), 1)
            q = (r >> 3) + 16 * t
            k = (q * 11) >> 5
            s = q - 3 * k
            k = jnp.minimum(k, 31)
            node = me >> k
            odd = (node & 1) == 1
            offset = jnp.where(
                odd,
                jnp.where(s == 0, odd_offsets[0], jnp.where(s == 1, odd_offsets[1], odd_offsets[2])),
                jnp.where(s == 0, even_offsets[0], jnp.where(s == 1, even_offsets[1], even_offsets[2])),
            )
            partner = node + offset
            count = devices >> k
            live = (partner >= 0) & (partner < count) & (k < top_levels)
            want = jnp.where(live, (count + partner) * 8 + (r & 7), -1)
            sources = jnp.dot((c == want).astype(f32).astype(bf16), whole, preferred_element_type=f32).astype(bf16)
            blocks = stacked(vrows_ref[heap + path_slots + 16 * t : heap + path_slots + 16 * t + 16, :])
            product = times_each(sources, blocks, spread, mask)
            terms.extend(product[8 * i : 8 * i + 8] for i in range(16))
        yield
        path_blocks = stacked(vrows_ref[heap : heap + path_slots, :])
        lane = lax.broadcasted_iota(jnp.int32, (8, 1024), 1)
        parent = None
        for k in range(top_levels - 1, -1, -1):
            value = terms[3 * k] + terms[3 * k + 1] + terms[3 * k + 2]
            if parent is not None:
                value = value + back_each(parent, path_blocks, gather, (lane & 15) == k)
            parent = value.astype(bf16).astype(f32)
            yield
        local_copy.wait()
        width = 2
        while width <= leaves:
            start = 2 * leaves - 2 * width
            if width >= 16:
                parts = []
                for g in range(width // 16):
                    blocks = stacked(local_ref[start + 16 * g : start + 16 * g + 16, :])
                    pair = doubled(parent[64 * g : 64 * g + 64])
                    parts.append(back_wide(pair, blocks, mask))
                wide = jnp.concatenate(parts, axis=0) if len(parts) > 1 else parts[0]
                parent = jnp.dot(wide, gather, preferred_element_type=f32)
            else:
                first = start - (2 * leaves - 16)
                blocks = stacked(last_rows(last_ref))
                pieces = [doubled(parent)]
                if first:
                    pieces.insert(0, jnp.zeros((8 * first, 64), f32))
                rest = 16 - first - width
                if rest:
                    pieces.append(jnp.zeros((8 * rest, 64), f32))
                parent = back_each(jnp.concatenate(pieces, axis=0), blocks, gather, mask)
                parent = parent[8 * first : 8 * (first + width)]
            width *= 2
            if width <= leaves:
                yield
        down_ref[...] = parent

    steps = tree()
    sums = []
    for g in range(groups):
        sums.append(coupling(g))
        for _ in range(2):
            next(steps, None)
    for _ in steps:
        pass
    for g in range(groups):
        down_ref[64 * g : 64 * g + 64, :] += sums[g]
    basis_copy.wait()

    def expand(step, _):
        for k in range(8):
            leaf = step * 8 + k
            mine = down_ref[pl.ds(pl.multiple_of(leaf * 8, 8), 8), :].astype(bf16)
            cols = pl.ds(pl.multiple_of(leaf * 256, 256), 256)
            out_ref[:, cols] = jnp.dot(mine, basis_ref[leaf], preferred_element_type=f32)
        return 0

    lax.fori_loop(0, leaves // 8, expand, 0, unroll=4)


def far_field(devices, place, ids, window, couple, upper, local, basis):
    leaves, rank, leaf_size = basis.shape
    top_levels = devices.bit_length() - 1
    rows = 2 * devices + 16 + -(-3 * top_levels // 16) * 16
    vmem = pl.BlockSpec(memory_space=pltpu.VMEM)
    return pl.pallas_call(
        lambda *refs: far_kernel(devices, *refs),
        grid=(1,),
        out_shape=jax.ShapeDtypeStruct((8, leaves * leaf_size), jnp.float32),
        in_specs=[pl.BlockSpec(memory_space=pltpu.SMEM)]
        + [vmem] * 6
        + [pl.BlockSpec((16, rank * rank), lambda g: (2 * leaves // 16 - 1, 0))]
        + [pl.BlockSpec(memory_space=pltpu.HBM)] * 4,
        out_specs=vmem,
        scratch_shapes=[
            pltpu.VMEM((8 * rank, 384), jnp.bfloat16),
            pltpu.VMEM((rows, 4096), jnp.bfloat16),
            pltpu.VMEM((8 * leaves, rank), jnp.float32),
            pltpu.VMEM(couple.shape, couple.dtype),
            pltpu.VMEM(upper.shape, upper.dtype),
            pltpu.VMEM(basis.shape, basis.dtype),
            pltpu.VMEM((2 * leaves - 16, rank * rank), jnp.bfloat16),
            pltpu.SemaphoreType.DMA((3 + leaves // 8,)),
        ],
        compiler_params=pltpu.CompilerParams(
            vmem_limit_bytes=VMEM_BYTES, dimension_semantics=("arbitrary",)
        ),
        cost_estimate=pl.CostEstimate(flops=2 * 2**28, bytes_accessed=16 * 2**20, transcendentals=0),
        name="far_field",
    )(place, ids, *window, local, local, couple, upper, basis)


def shards(
    points,
    vectors,
    near_list,
    near_count,
    couple_list,
    leaf_basis,
    local_transfer,
    couple_block,
    upper_transfer,
    upper_couple,
):
    devices = lax.axis_size(AXES)
    my_index = lax.axis_index(AXES).astype(jnp.int32)
    leaves, rank, leaf_size = leaf_basis.shape
    couple_slots = couple_list.shape[1]

    local_near = near_list - (my_index - 1) * leaves
    slot = jnp.arange(near_list.shape[1], dtype=jnp.int32)[None, :]
    lists = jnp.where(slot < near_count[:, None], local_near + 1, 0).reshape(-1)
    own = pack_rows(points, vectors, lists)
    place = my_index.reshape(1)
    left = from_behind(own, 1)
    right = from_behind(own, -1)
    local = local_transfer[0]
    coef, upper = up_tree(devices, own, upper_transfer, upper_couple.transpose(1, 0, 2), leaf_basis, local)
    window = [from_behind(coef, d) if d else coef for d in range(REACH, -REACH - 1, -1)]
    upper, left, right = lax.optimization_barrier((upper, left, right))
    upper = lax.all_to_all(upper, AXES, 0, 0, tiled=True)

    near = near_field(devices, place, leaves, near_list.shape[1], left, own, right)
    for_left, near, for_right, upper, window = lax.optimization_barrier((*near, upper, window))
    from_right = from_behind(for_left, -1)
    from_left = from_behind(for_right, 1)

    ids = (couple_list - (my_index - REACH) * leaves).reshape(leaves // 8, 8 * couple_slots)
    couple = couple_block.reshape(leaves * couple_slots, rank * rank)
    far = far_field(
        devices, place, ids, window, couple, upper.reshape(devices * 8, -1), local, leaf_basis
    )
    return far + near + (from_left + from_right)


def solution(mesh):
    placed = (
        P(None, AXES),
        P(None, AXES),
        P(AXES, None),
        P(AXES),
        P(AXES, None),
        P(AXES, None, None),
        P(AXES, None, None),
        P(AXES, None, None),
        P(AXES, None),
        P(AXES, None, None),
    )
    return jax.shard_map(shards, mesh=mesh, in_specs=placed, out_specs=P(None, AXES), check_vma=False)
```
